32 devices in a mesh: vol: 4 (over z), row: 4 (over y, core), col: 2 (over x).
Axes of the slice: x: 2, y: 2, z: 4, core: 2. Of those that a mesh axis runs over, the one named last changes fastest.
Arguments:
- vol_rhs: bfloat16 [64, 49152], P(None, ('vol', 'row', 'col')), may hold values from -6 to 6
- surf_rhs: bfloat16 [64, 4096], P(None, ('vol', 'row', 'col')), may hold values from -6 to 6
- vol_blocks: bfloat16 [384, 7, 128, 128], P(('vol', 'row', 'col')), may hold values from -0.1875 to 0.1875
- vol_cols: int32 [384, 7], P(('vol', 'row', 'col')), may hold values from 0 to 11, as said below
- coupling: bfloat16 [128, 128, 128], P(('vol', 'row', 'col')), may hold values from -0.5 to 0.5
- trace_map: int32 [128], P(('vol', 'row', 'col')), may hold values from 0 to 3
- bnd_count: int32 [32], P(('vol', 'row', 'col')), may hold values from 1 to 4
- surf_inverse: bfloat16 [32, 128, 128], P(('vol', 'row', 'col')), may hold values from -0.5 to 0.5
- near_blocks: bfloat16 [32, 2, 4, 128, 128], P(('vol', 'row'), 'col'), may hold values from -0.1875 to 0.1875
- near_cols: int32 [32, 2, 4], P(('vol', 'row'), 'col'), may hold values from 0 to 15
- far_u: bfloat16 [2, 32, 4096], P('col', None, ('vol', 'row')), may hold values from -1 to 1
- far_v: bfloat16 [16, 2, 32, 2048], P(('vol', 'row'), 'col'), may hold values from -0.125 to 0.125
Outputs:
- vol_field: float32 [64, 49152], P(None, ('vol', 'row', 'col'))
- surf_field: float32 [64, 4096], P(None, ('vol', 'row', 'col'))
The draws below stay inside these ranges and needn't reach their ends.
Inputs may be any that keep to these rules, and one draw needn't show every extreme that they name: `vol_cols`: row b names 7 different blocks of its own subdomain, the first being b mod 12.
All inputs are finite; a program needn't handle non-finite values.
Results may differ from the reference program's by a relative error of at most 0.01.
Values may be sent and summed in bfloat16 or wider, within the bound.
No kernel may reach another device: no remote copies, remote signals or barrier semaphores. Data moves between devices by JAX's collectives and lax.ppermute only.
A program may use at most 64 MiB of HBM per device.

```python
import jax
import jax.numpy as jnp
from jax import lax

ANG = 64
VBLK = 12
SBLK = 1
BS = 128
NNZV = 7
NBND = 4
NEAR = 4
RANK = 32
ITERS = 2
VOLUME = 49152
SURFACE = 4096
VOL_BLOCKS = 384
SURF_BLOCKS = 32
BND_SLOTS = 128
GROUP_ROWS = 2048
N_VOL = 4
N_ROW = 4
N_COL = 2
DEVICES = 32


def draw_vol_cols(key, part):
    row_keys = jax.random.split(key, VOL_BLOCKS)

    def offsets_of(row_key):
        return jax.random.permutation(row_key, VBLK - 1)[:NNZV - 1].astype(jnp.int32) + 1
    offsets = jax.vmap(offsets_of)(row_keys)
    own_block = jnp.arange(VOL_BLOCKS, dtype=jnp.int32) % VBLK
    leading = jnp.zeros((VOL_BLOCKS, 1), jnp.int32)
    shifts = jnp.concatenate([leading, offsets], axis=1)
    return ((own_block[:, None] + shifts) % VBLK).astype(jnp.int32)


def touch_ends(entries, rng, low, high):
    place = [jax.random.randint(jax.random.fold_in(rng, axis), (), 0, length) for axis, length in enumerate(entries.shape)]
    widest = entries.shape.index(max(entries.shape))
    beside = place[:widest] + [(place[widest] + 1) % entries.shape[widest]] + place[widest + 1:]
    return entries.at[tuple(place)].set(low).at[tuple(beside)].set(high)


def levels(key, extent, cuts, least, largest):
    level, own = 1.0, jax.random.fold_in(key, 6)
    for position, parts in cuts:
        steps = jnp.exp(jax.random.uniform(jax.random.fold_in(own, position), (parts,), jnp.float32, least / len(cuts), largest / len(cuts)))
        level = level * jnp.repeat(steps, extent[position] // parts).reshape([-1 if axis == position else 1 for axis in range(len(extent))])
    return level


def bell_draw(key, extent, deviation, reach, cuts=(), held_as=jnp.bfloat16):
    entries = deviation * jax.random.normal(key, extent, jnp.float32)
    if cuts:
        entries = entries * levels(key, extent, cuts, -0.22, 0.18)
    return jnp.clip(entries, -reach, reach).astype(held_as)


def setup_inputs(seed: int = 0) -> dict:
    seeds = jax.random.split(jax.random.key(seed), 13)
    return {
        "vol_rhs": bell_draw(seeds[0], (ANG, VOLUME), 1.0, 6.0, ((1, 32),)),
        "surf_rhs": bell_draw(seeds[1], (ANG, SURFACE), 1.0, 6.0, ((1, 32),)),
        "vol_blocks": bell_draw(seeds[2], (VOL_BLOCKS, NNZV, BS, BS), (NNZV * BS) ** -0.5, 0.1875, ((0, 32),)),
        "vol_cols": draw_vol_cols(jax.random.fold_in(seeds[12], 71), 0),
        "coupling": bell_draw(seeds[4], (BND_SLOTS, BS, BS), BS ** -0.5, 0.5, ((0, 32),)),
        "trace_map": touch_ends(jax.random.randint(seeds[5], (BND_SLOTS,), 0, N_VOL * SBLK), jax.random.fold_in(seeds[5], 1), 0, (N_VOL * SBLK) - 1).astype(jnp.int32),
        "bnd_count": touch_ends(jax.random.randint(seeds[6], (DEVICES,), 1, NBND + 1), jax.random.fold_in(seeds[6], 1), 1, NBND).astype(jnp.int32),
        "surf_inverse": bell_draw(seeds[7], (SURF_BLOCKS, BS, BS), BS ** -0.5, 0.5, ((0, 32),)),
        "near_blocks": bell_draw(seeds[8], (SURF_BLOCKS, N_COL, NEAR, BS, BS), (N_COL * NEAR * BS) ** -0.5, 0.1875, ((0, 16), (1, 2))),
        "near_cols": touch_ends(jax.random.randint(seeds[9], (SURF_BLOCKS, N_COL, NEAR), 0, N_VOL * N_ROW * SBLK), jax.random.fold_in(seeds[9], 1), 0, (N_VOL * N_ROW * SBLK) - 1).astype(jnp.int32),
        "far_u": bell_draw(seeds[10], (N_COL, RANK, SURFACE), RANK ** -0.5, 1.0, ((0, 2), (2, 16))),
        "far_v": bell_draw(seeds[11], (N_VOL * N_ROW, N_COL, RANK, GROUP_ROWS), GROUP_ROWS ** -0.5, 0.125, ((0, 16), (1, 2))),
    }


def halved(value):
    return lax.optimization_barrier(value.astype(jnp.bfloat16))


def volume_solve(field, sub_blocks, sub_columns):
    def subdomain_solve(member):
        local_field, blocks, columns = member
        picked = jnp.take(local_field, columns, axis=1)
        return jnp.einsum("abnk,bnik->abi", picked.astype(jnp.float32), blocks.astype(jnp.float32))

    result = lax.map(subdomain_solve, (jnp.transpose(field, (1, 0, 2, 3)), sub_blocks, sub_columns))
    return jnp.transpose(result, (1, 0, 2, 3))


def reference(vol_rhs, surf_rhs, vol_blocks, vol_cols, coupling, trace_map, bnd_count, surf_inverse, near_blocks, near_cols, far_u, far_v):
    devices = N_VOL * N_ROW * N_COL
    groups = N_ROW * N_COL
    row_groups = N_VOL * N_ROW
    piece_rows = SBLK * BS
    block_slots = N_VOL * SBLK
    sub_blocks = vol_blocks.reshape(devices, VBLK, NNZV, BS, BS)
    sub_columns = vol_cols.reshape(devices, VBLK, NNZV)
    couple = coupling.reshape(devices, NBND, BS, BS).astype(jnp.float32)
    slot_maps = trace_map.reshape(devices, NBND)
    slot_alive = (jnp.arange(NBND, dtype=jnp.int32)[None, :] < bnd_count[:, None]).astype(jnp.float32)
    selector = (slot_maps[:, :, None] == jnp.arange(block_slots, dtype=jnp.int32)[None, None, :]).astype(jnp.float32)
    selector = selector.reshape(N_VOL, groups, NBND, block_slots)
    inverse = surf_inverse.reshape(devices, SBLK, BS, BS).astype(jnp.float32)
    rhs_vol = vol_rhs.astype(jnp.float32).reshape(ANG, devices, VBLK, BS)
    rhs_surf = surf_rhs.astype(jnp.float32)
    near_all = near_blocks.reshape(row_groups, N_COL * SBLK, N_COL, NEAR, BS, BS)
    near_ids = near_cols.reshape(row_groups, N_COL * SBLK, N_COL, NEAR)
    u_parts = jnp.transpose(far_u.reshape(N_COL, RANK, row_groups, N_COL * piece_rows), (2, 0, 1, 3))
    group_of = jnp.arange(devices, dtype=jnp.int32) % groups
    col_index = jnp.arange(N_COL, dtype=jnp.int32)[None, :, None]

    def surface_solve(field):
        blocks = field.astype(jnp.float32).reshape(ANG, devices, SBLK, BS)
        return jnp.einsum("adbk,dbik->adbi", blocks, inverse).reshape(ANG, devices * piece_rows)

    volume = volume_solve(vol_rhs.reshape(ANG, devices, VBLK, BS), sub_blocks, sub_columns)
    surface = surface_solve(surf_rhs)
    for iteration in range(ITERS):
        x_half = halved(volume)
        s_half = halved(surface)
        grouped = jnp.transpose(s_half.reshape(ANG, N_VOL, groups, SBLK, BS), (2, 0, 1, 3, 4)).reshape(groups, ANG, block_slots, BS)
        picked = grouped[group_of[:, None], :, slot_maps, :]
        current = jnp.einsum("djak,djik->adji", picked.astype(jnp.float32), couple) * slot_alive[None, :, :, None]
        padding = jnp.zeros((ANG, devices, VBLK - NBND, BS), jnp.float32)
        resid_vol = halved(rhs_vol - jnp.concatenate([current, padding], axis=2))
        boundary = x_half[:, :, :NBND, :].astype(jnp.float32)
        contrib = jnp.einsum("adji,djik->adjk", boundary, couple) * slot_alive[None, :, :, None]
        traced = jnp.einsum("avgjk,vgjm->agmk", contrib.reshape(ANG, N_VOL, groups, NBND, BS), selector)
        traced = jnp.transpose(traced.reshape(ANG, groups, N_VOL, SBLK, BS), (0, 2, 1, 3, 4)).reshape(ANG, devices * piece_rows)
        column_half = jnp.transpose(s_half.reshape(ANG, row_groups, N_COL, piece_rows), (2, 0, 1, 3)).reshape(N_COL, ANG, row_groups * piece_rows)
        column_wide = column_half.astype(jnp.float32)
        column_blocks = column_half.reshape(N_COL, ANG, row_groups * SBLK, BS)

        def group_rows(member):
            blocks, indices, v_factor, u_factor = member
            gathered = column_blocks[col_index, :, indices, :]
            near_term = jnp.einsum("bcnak,bcnik->abi", gathered.astype(jnp.float32), blocks.astype(jnp.float32))
            coeffs = jnp.einsum("cak,cqk->caq", column_wide, v_factor.astype(jnp.float32))
            coeffs = halved(coeffs).astype(jnp.float32)
            far_term = jnp.einsum("caq,cqi->ai", coeffs, u_factor.astype(jnp.float32))
            return near_term.reshape(ANG, N_COL * piece_rows) + far_term

        integral = lax.map(group_rows, (near_all, near_ids, far_v, u_parts))
        integral = jnp.transpose(integral, (1, 0, 2)).reshape(ANG, devices * piece_rows)
        resid_surf = halved(rhs_surf - integral - traced)
        volume = volume_solve(resid_vol, sub_blocks, sub_columns)
        surface = surface + surface_solve(resid_surf)
    return volume.reshape(ANG, devices * VBLK * BS), surface
```

```python
import functools

import jax
import jax.numpy as jnp
from jax import lax
from jax.experimental import pallas as pl
from jax.experimental.pallas import tpu as pltpu
from jax.sharding import PartitionSpec as P

ITERS = 2
UNROLL = 16
F32 = jnp.float32
HALF = jnp.bfloat16


def by_rows(a, b):
    return lax.dot_general(a, b, (((1,), (1,)), ((), ())), preferred_element_type=F32)


def by_cols(a, b):
    return lax.dot_general(a, b, (((1,), (0,)), ((), ())), preferred_element_type=F32)


def block(start, size):
    return pl.ds(pl.multiple_of(start * size, size), size)


def slot_of(index, here, count):
    return lax.rem(index - here + count, count)


def block_row(read, blocks, columns, row):
    terms = blocks.shape[1]
    field = jnp.concatenate([read(columns[row, n]) for n in range(terms)], axis=1)
    inverse = jnp.concatenate([blocks[row, n] for n in range(terms)], axis=1)
    return by_rows(field, inverse)


def add_traces(total, boundary, coupling, trace_map, bnd_count, axis):
    count = total.shape[0]
    bs = coupling.shape[-1]
    subs = total.shape[2] // bs
    here = lax.axis_index(axis)
    for j in range(coupling.shape[0]):
        alive = (j < bnd_count[0]).astype(F32)
        contrib = by_cols(boundary(j), coupling[j]) * alive
        target = trace_map[j]
        slot = slot_of(target // subs, here, count)
        where = (slot, slice(None), block(lax.rem(target, subs), bs))
        total[where] = total[where] + contrib


def residual_blocks(resid, vol_rhs, group, coupling, trace_map, bnd_count, axis, count):
    bs = coupling.shape[-1]
    angles = vol_rhs.shape[0]
    subs = group.shape[1] // bs
    here = lax.axis_index(axis)
    for j in range(coupling.shape[0]):
        alive = (j < bnd_count[0]).astype(F32)
        target = trace_map[j]
        slot = slot_of(here, target // subs, count)
        picked = group[block(slot, angles), block(lax.rem(target, subs), bs)]
        current = by_rows(picked, coupling[j]) * alive
        rhs = vol_rhs[:, j * bs : (j + 1) * bs].astype(F32)
        resid[j] = (rhs - current).astype(HALF)


def send_out(payloads, half, total):
    angles = half.shape[0]
    for k, payload in enumerate(payloads):
        payload[0:angles, :] = half
        payload[angles : 2 * angles, :] = total[k + 1].astype(HALF)


def start_kernel(axis, refs):
    (surf_rhs, surf_inverse, vol_rhs, blocks, coupling, columns, trace_map, bnd_count) = refs[:8]
    surface, half_out, own_trace = refs[8:11]
    payloads, total = refs[11:-1], refs[-1]
    bs = coupling.shape[-1]
    for b in range(surf_inverse.shape[0]):
        cols = slice(b * bs, (b + 1) * bs)
        surface[:, cols] = by_rows(surf_rhs[:, cols], surf_inverse[b])
    half = surface[...].astype(HALF)
    half_out[...] = half
    total[...] = jnp.zeros_like(total)

    def read(col):
        return vol_rhs[:, block(col, bs)]

    def boundary(j):
        return block_row(read, blocks, columns, j).astype(HALF)

    add_traces(total, boundary, coupling, trace_map, bnd_count, axis)
    own_trace[...] = total[0]
    send_out(payloads, half, total)


def boundary_kernel(axis, refs):
    (group, vol_rhs, blocks, coupling, columns, trace_map, bnd_count, total, field) = refs
    bs = coupling.shape[-1]
    slots = coupling.shape[0]
    count = total.shape[0]
    for b in range(slots, vol_rhs.shape[1] // bs):
        field[b] = vol_rhs[:, b * bs : (b + 1) * bs]
    residual_blocks(field, vol_rhs, group, coupling, trace_map, bnd_count, axis, count)
    total[...] = jnp.zeros_like(total)

    def boundary(j):
        return block_row(lambda col: field[col], blocks, columns, j).astype(HALF)

    add_traces(total, boundary, coupling, trace_map, bnd_count, axis)


def volume_kernel(axis, count, refs):
    (group, vol_rhs, blocks, coupling, columns, trace_map, bnd_count, volume, field) = refs
    bs = coupling.shape[-1]
    for b in range(coupling.shape[0], vol_rhs.shape[1] // bs):
        field[b] = vol_rhs[:, b * bs : (b + 1) * bs]
    residual_blocks(field, vol_rhs, group, coupling, trace_map, bnd_count, axis, count)
    for b in range(blocks.shape[0]):
        volume[:, b * bs : (b + 1) * bs] = block_row(lambda col: field[col], blocks, columns, b)


def dense_kernel(vol_size, row_size, col_size, refs):
    near_blocks, near_cols, far_u, far_v, dense, work = refs
    bs = near_blocks.shape[-1]
    rows = near_blocks.shape[0]
    subs = rows // col_size
    vol, row, col = (lax.axis_index(name) for name in ("vol", "row", "col"))

    def place(number):
        piece = number // subs
        row_slot = slot_of(row, lax.rem(piece, row_size), row_size)
        vol_slot = slot_of(vol, piece // row_size, vol_size)
        return (row_slot * vol_size + vol_slot) * subs + lax.rem(number, subs)

    total = vol_size * row_size * subs
    for k in range(col_size):
        piece = lax.rem(col + k, col_size)
        for sub in range(subs):
            b = piece * subs + sub
            u = far_u[0, :, block(b, bs)]

            def far(number, _):
                v = far_v[0, 0, :, block(number, bs)]
                work[block(place(number), bs), :] = lax.dot_general(
                    v, u, (((0,), (0,)), ((), ())), preferred_element_type=F32
                )
                return _

            lax.fori_loop(0, total, far, 0, unroll=min(total, UNROLL))
            for n in range(near_blocks.shape[2]):
                where = (block(place(near_cols[b, 0, n]), bs), slice(None))
                work[where] = work[where] + near_blocks[b, 0, n].astype(F32).T
            at = (k * subs + sub) * bs
            dense[:, at : at + bs] = work[...].astype(HALF)


def integral_kernel(row_size, vol_size, refs):
    groups, dense, outs = refs[:row_size], refs[row_size], refs[row_size + 1 :]
    angles, width = groups[0].shape[0] // vol_size, groups[0].shape[1]
    field = jnp.concatenate(
        [g[k * angles : (k + 1) * angles, :] for g in groups for k in range(vol_size)], axis=1
    )
    part = by_cols(field, dense[...])
    for k, out in enumerate(outs):
        out[...] = part[:, k * width : (k + 1) * width].astype(out.dtype)


def update_surface(surface, surf_rhs, surf_inverse, integral, traces, sums, received, out):
    bs = surf_inverse.shape[-1]
    angles = surf_rhs.shape[0]
    taken = integral[...] + traces
    for s in sums:
        taken = taken + s[...].astype(F32)
    for r in received:
        taken = taken + r[angles : 2 * angles, :].astype(F32)
    resid = (surf_rhs[...].astype(F32) - taken).astype(HALF)
    for b in range(surf_inverse.shape[0]):
        cols = slice(b * bs, (b + 1) * bs)
        out[:, cols] = surface[:, cols] + by_rows(resid[:, cols], surf_inverse[b])


def step_kernel(sums, received, refs):
    surface, surf_rhs, surf_inverse, integral, own_trace, total = refs[:6]
    sums, refs = refs[6 : 6 + sums], refs[6 + sums :]
    received, refs = refs[:received], refs[received:]
    out, half_out, next_trace = refs[:3]
    payloads = refs[3:]
    update_surface(
        surface, surf_rhs, surf_inverse, integral, own_trace[...], sums, received, out
    )
    half = out[...].astype(HALF)
    half_out[...] = half
    next_trace[...] = total[0]
    send_out(payloads, half, total)


def last_kernel(sums, received, refs):
    surface, surf_rhs, surf_inverse, integral, own_trace = refs[:5]
    out = refs[-1]
    sums, received = refs[5 : 5 + sums], refs[5 + sums : 5 + sums + received]
    update_surface(
        surface, surf_rhs, surf_inverse, integral, own_trace[...], sums, received, out
    )


VMEM = pl.BlockSpec(memory_space=pltpu.VMEM)
SMEM = pl.BlockSpec(memory_space=pltpu.SMEM)


def call(body, name, in_specs, outs, flops, moved, scratch=()):
    def kernel(*refs):
        body(refs)

    return pl.pallas_call(
        kernel,
        name=name,
        out_shape=outs,
        in_specs=in_specs,
        out_specs=[VMEM] * len(outs),
        scratch_shapes=list(scratch),
        cost_estimate=pl.CostEstimate(flops=flops, bytes_accessed=moved, transcendentals=0),
        compiler_params=pltpu.CompilerParams(vmem_limit_bytes=48 << 20),
    )


def shifted(value, axis, shift):
    size = lax.axis_size(axis)
    return lax.ppermute(value, axis, [(i, (i + shift) % size) for i in range(size)])


def local(
    vol_rhs,
    surf_rhs,
    vol_blocks,
    vol_cols,
    coupling,
    trace_map,
    bnd_count,
    surf_inverse,
    near_blocks,
    near_cols,
    far_u,
    far_v,
):
    angles, width = surf_rhs.shape
    vol_count, terms, bs, _ = vol_blocks.shape
    slots = coupling.shape[0]
    nv, nr, nc = (lax.axis_size(a) for a in ("vol", "row", "col"))
    piece = (angles, width)
    product = 2 * angles * bs * bs

    def shape(dims, dtype):
        return jax.ShapeDtypeStruct(dims, dtype)

    boundary_blocks = vol_blocks[:slots]
    tables = (vol_cols, trace_map, bnd_count)
    payload_shapes = [shape((2 * angles, width), HALF)] * (nv - 1)
    totals = pltpu.VMEM((nv,) + piece, F32)
    field = pltpu.VMEM((vol_count, angles, bs), HALF)

    surface, half, own_trace, *payloads = call(
        functools.partial(start_kernel, "vol"),
        "start",
        [VMEM] * 3 + [VMEM] * 2 + [SMEM] * 3,
        [shape(piece, F32), shape(piece, HALF), shape(piece, F32)] + payload_shapes,
        product * slots * (terms + 1),
        2 * bs * bs * slots * (terms + 1),
        [totals],
    )(surf_rhs, surf_inverse, vol_rhs, boundary_blocks, coupling, *tables)

    (dense,) = call(
        functools.partial(dense_kernel, nv, nr, nc),
        "dense",
        [VMEM, SMEM, VMEM, VMEM],
        [shape((nv * nr * width, nc * width), HALF)],
        product * nv * nr * nc,
        4 * nv * nr * nc * bs * bs,
        [pltpu.VMEM((nv * nr * width, bs), F32)],
    )(near_blocks, near_cols, far_u, far_v)

    for iteration in range(ITERS):
        received = [shifted(payloads[k - 1], "vol", k) for k in range(1, nv)]
        group = jnp.concatenate([half] + [r[:angles] for r in received], axis=0)
        groups = [group] + [shifted(group, "row", k) for k in range(1, nr)]
        last = iteration == ITERS - 1
        if last:
            (volume,) = call(
                functools.partial(volume_kernel, "vol", nv),
                "volume",
                [VMEM] * 4 + [SMEM] * 3,
                [shape((angles, vol_count * bs), F32)],
                product * vol_count * terms,
                2 * bs * bs * vol_count * terms,
                [field],
            )(group, vol_rhs, vol_blocks, coupling, *tables)
        else:
            (total,) = call(
                functools.partial(boundary_kernel, "vol"),
                "boundary",
                [VMEM] * 2 + [VMEM] * 2 + [SMEM] * 3,
                [shape((nv,) + piece, F32)],
                product * slots * (terms + 2),
                2 * bs * bs * slots * (terms + 1),
                [field],
            )(group, vol_rhs, boundary_blocks, coupling, *tables)
        integral, *parts = call(
            functools.partial(integral_kernel, nr, nv),
            "integral",
            [VMEM] * (nr + 1),
            [shape(piece, F32)] + [shape(piece, HALF)] * (nc - 1),
            product * nv * nr * nc,
            2 * nv * nr * nc * width * width,
        )(*groups, dense)
        sums = [shifted(parts[k - 1], "col", k) for k in range(1, nc)]
        if last:
            (surface,) = call(
                functools.partial(last_kernel, nc - 1, nv - 1),
                "last",
                [VMEM] * (5 + nc - 1 + nv - 1),
                [shape(piece, F32)],
                product,
                1 << 17,
            )(surface, surf_rhs, surf_inverse, integral, own_trace, *sums, *received)
        else:
            surface, half, own_trace, *payloads = call(
                functools.partial(step_kernel, nc - 1, nv - 1),
                "step",
                [VMEM] * (6 + nc - 1 + nv - 1),
                [shape(piece, F32), shape(piece, HALF), shape(piece, F32)] + payload_shapes,
                product,
                1 << 17,
            )(surface, surf_rhs, surf_inverse, integral, own_trace, total, *sums, *received)
    return volume, surface


def solution(mesh):
    everywhere = ("vol", "row", "col")
    in_specs = (
        P(None, everywhere),
        P(None, everywhere),
        P(everywhere, None, None, None),
        P(everywhere, None),
        P(everywhere, None, None),
        P(everywhere),
        P(everywhere),
        P(everywhere, None, None),
        P(("vol", "row"), "col", None, None, None),
        P(("vol", "row"), "col", None),
        P("col", None, ("vol", "row")),
        P(("vol", "row"), "col", None, None),
    )
    out_specs = (P(None, everywhere), P(None, everywhere))
    return jax.shard_map(local, mesh=mesh, in_specs=in_specs, out_specs=out_specs, check_vma=False)
```

```python
import functools

import jax
import jax.numpy as jnp
from jax import lax
from jax.experimental import pallas as pl
from jax.experimental.pallas import tpu as pltpu
from jax.sharding import PartitionSpec as P

ITERS = 2
UNROLL = 16
F32 = jnp.float32
HALF = jnp.bfloat16


def by_rows(a, b):
    return lax.dot_general(a, b, (((1,), (1,)), ((), ())), preferred_element_type=F32)


def by_cols(a, b):
    return lax.dot_general(a, b, (((1,), (0,)), ((), ())), preferred_element_type=F32)


def block(start, size):
    return pl.ds(pl.multiple_of(start * size, size), size)


def slot_of(index, here, count):
    return lax.rem(index - here + count, count)


def block_row(read, blocks, columns, row):
    terms = blocks.shape[1]
    field = jnp.concatenate([read(columns[n, row]) for n in range(terms)], axis=1)
    inverse = jnp.concatenate([blocks[row, n] for n in range(terms)], axis=1)
    return by_rows(field, inverse)


def add_traces(total, boundary, coupling, trace_map, bnd_count, axis):
    count = total.shape[0]
    bs = coupling.shape[-1]
    subs = total.shape[2] // bs
    here = lax.axis_index(axis)
    for j in range(coupling.shape[0]):
        alive = (j < bnd_count[0]).astype(F32)
        contrib = by_cols(boundary(j), coupling[j]) * alive
        target = trace_map[j]
        slot = slot_of(target // subs, here, count)
        where = (slot, slice(None), block(lax.rem(target, subs), bs))
        total[where] = total[where] + contrib


def residual_blocks(resid, vol_rhs, group, coupling, trace_map, bnd_count, axis, count):
    bs = coupling.shape[-1]
    angles = vol_rhs.shape[0]
    subs = group.shape[1] // bs
    here = lax.axis_index(axis)
    for j in range(coupling.shape[0]):
        alive = (j < bnd_count[0]).astype(F32)
        target = trace_map[j]
        slot = slot_of(here, target // subs, count)
        picked = group[block(slot, angles), block(lax.rem(target, subs), bs)]
        current = by_rows(picked, coupling[j]) * alive
        rhs = vol_rhs[:, j * bs : (j + 1) * bs].astype(F32)
        resid[j] = (rhs - current).astype(HALF)


def send_out(payloads, half, total):
    angles = half.shape[0]
    for k, payload in enumerate(payloads):
        payload[0:angles, :] = half
        payload[angles : 2 * angles, :] = total[k + 1].astype(HALF)


def start_kernel(axis, outs, kept, refs):
    bnd_count, operands, refs = refs[0], refs[1 : 8 + kept], refs[8 + kept :]
    surface, half_out, own_trace, *payloads = refs[:outs]
    copied, refs = refs[outs : outs + kept + 2], refs[outs + kept + 2 :]
    surf_rhs, surf_inverse, vol_rhs, blocks, coupling, columns, trace_map, total, sems = refs
    slots = coupling.shape[0]
    bs = coupling.shape[-1]
    count = iter(range(sems.shape[0]))

    def copy(source, to):
        started = pltpu.make_async_copy(source, to, sems.at[next(count)])
        started.start()
        return started

    tables = [copy(operands[5 + i], t) for i, t in enumerate((columns, trace_map))]
    first = [copy(operands[0], surf_rhs), copy(operands[1], surf_inverse)]
    tables.append(copy(operands[2], vol_rhs))
    rows = [copy(operands[3].at[j], blocks.at[j]) for j in range(slots)]
    last = copy(operands[4], coupling)
    later = [copy(operands[5 + i], t) for i, t in enumerate(copied)]
    total[...] = jnp.zeros_like(total)
    for c in first:
        c.wait()
    for b in range(surf_inverse.shape[0]):
        cols = slice(b * bs, (b + 1) * bs)
        surface[:, cols] = by_rows(surf_rhs[:, cols], surf_inverse[b])
    half = surface[...].astype(HALF)
    half_out[...] = half
    for c in tables:
        c.wait()
    solved = []
    for j in range(slots):
        rows[j].wait()
        read = lambda col: vol_rhs[:, block(col, bs)]
        solved.append(block_row(read, blocks, columns, j).astype(HALF))
    last.wait()
    add_traces(total, lambda j: solved[j], coupling, trace_map, bnd_count, axis)
    own_trace[...] = total[0]
    send_out(payloads, half, total)
    for c in later:
        c.wait()


def boundary_kernel(axis, refs):
    (group, vol_rhs, blocks, coupling, columns, trace_map, bnd_count, total, field) = refs
    bs = coupling.shape[-1]
    slots = coupling.shape[0]
    count = total.shape[0]
    for b in range(slots, vol_rhs.shape[1] // bs):
        field[b] = vol_rhs[:, b * bs : (b + 1) * bs]
    residual_blocks(field, vol_rhs, group, coupling, trace_map, bnd_count, axis, count)
    total[...] = jnp.zeros_like(total)

    def boundary(j):
        return block_row(lambda col: field[col], blocks, columns, j).astype(HALF)

    add_traces(total, boundary, coupling, trace_map, bnd_count, axis)


def early_kernel(axis, count, refs):
    (group, vol_rhs, blocks, coupling, columns, trace_map, bnd_count, early, field) = refs
    bs = coupling.shape[-1]
    for b in range(coupling.shape[0], vol_rhs.shape[1] // bs):
        field[b] = vol_rhs[:, b * bs : (b + 1) * bs]
    residual_blocks(field, vol_rhs, group, coupling, trace_map, bnd_count, axis, count)
    for b in range(early.shape[1] // bs):
        early[:, b * bs : (b + 1) * bs] = block_row(lambda col: field[col], blocks, columns, b)


def late_kernel(refs):
    early, field, blocks, columns, volume = refs
    bs = field.shape[-1]
    first = early.shape[1] // bs
    volume[:, : first * bs] = early[...]
    for b in range(first, blocks.shape[0]):
        volume[:, b * bs : (b + 1) * bs] = block_row(lambda col: field[col], blocks, columns, b)


def dense_kernel(vol_size, row_size, col_size, refs):
    near_blocks, near_cols, far_u, far_v, dense, work = refs
    bs = near_blocks.shape[-1]
    rows = near_blocks.shape[0]
    subs = rows // col_size
    vol, row, col = (lax.axis_index(name) for name in ("vol", "row", "col"))

    def place(number):
        piece = number // subs
        row_slot = slot_of(row, lax.rem(piece, row_size), row_size)
        vol_slot = slot_of(vol, piece // row_size, vol_size)
        return (row_slot * vol_size + vol_slot) * subs + lax.rem(number, subs)

    total = vol_size * row_size * subs
    for k in range(col_size):
        piece = lax.rem(col + k, col_size)
        for sub in range(subs):
            b = piece * subs + sub
            u = far_u[0, :, block(b, bs)]

            def far(number, _):
                v = far_v[0, 0, :, block(number, bs)]
                work[block(place(number), bs), :] = lax.dot_general(
                    v, u, (((0,), (0,)), ((), ())), preferred_element_type=F32
                )
                return _

            lax.fori_loop(0, total, far, 0, unroll=min(total, UNROLL))
            for n in range(near_blocks.shape[2]):
                where = (block(place(near_cols[b, 0, n]), bs), slice(None))
                work[where] = work[where] + near_blocks[b, 0, n].astype(F32).T
            at = (k * subs + sub) * bs
            dense[:, at : at + bs] = work[...].astype(HALF)


def integral_kernel(row_size, vol_size, refs):
    groups, dense, outs = refs[:row_size], refs[row_size], refs[row_size + 2 :]
    angles, width = groups[0].shape[0] // vol_size, groups[0].shape[1]
    field = jnp.concatenate(
        [g[k * angles : (k + 1) * angles, :] for g in groups for k in range(vol_size)], axis=1
    )
    part = by_cols(field, dense[...])
    for k, out in enumerate(outs):
        out[...] = part[:, k * width : (k + 1) * width].astype(out.dtype)


def update_surface(surface, surf_rhs, surf_inverse, integral, traces, sums, received, out):
    bs = surf_inverse.shape[-1]
    angles = surf_rhs.shape[0]
    taken = integral[...] + traces
    for s in sums:
        taken = taken + s[...].astype(F32)
    for r in received:
        taken = taken + r[angles : 2 * angles, :].astype(F32)
    resid = (surf_rhs[...].astype(F32) - taken).astype(HALF)
    for b in range(surf_inverse.shape[0]):
        cols = slice(b * bs, (b + 1) * bs)
        out[:, cols] = surface[:, cols] + by_rows(resid[:, cols], surf_inverse[b])


def step_kernel(sums, received, refs):
    surface, surf_rhs, surf_inverse, integral, own_trace, total = refs[:6]
    sums, refs = refs[6 : 6 + sums], refs[6 + sums :]
    received, refs = refs[:received], refs[received:]
    out, half_out, next_trace = refs[:3]
    payloads = refs[3:]
    update_surface(
        surface, surf_rhs, surf_inverse, integral, own_trace[...], sums, received, out
    )
    half = out[...].astype(HALF)
    half_out[...] = half
    next_trace[...] = total[0]
    send_out(payloads, half, total)


def last_kernel(sums, received, refs):
    surface, surf_rhs, surf_inverse, integral, own_trace = refs[:5]
    out = refs[-1]
    sums, received = refs[5 : 5 + sums], refs[5 + sums : 5 + sums + received]
    update_surface(
        surface, surf_rhs, surf_inverse, integral, own_trace[...], sums, received, out
    )


VMEM = pl.BlockSpec(memory_space=pltpu.VMEM)
SMEM = pl.BlockSpec(memory_space=pltpu.SMEM)


ANY = pl.BlockSpec(memory_space=pl.ANY)
HBM = pl.BlockSpec(memory_space=pltpu.HBM)


def call(body, name, in_specs, outs, flops, moved, scratch=()):
    def kernel(*refs):
        body(refs)

    return pl.pallas_call(
        kernel,
        name=name,
        out_shape=outs,
        in_specs=in_specs,
        out_specs=[VMEM] * len(outs),
        scratch_shapes=list(scratch),
        cost_estimate=pl.CostEstimate(flops=flops, bytes_accessed=moved, transcendentals=0),
        compiler_params=pltpu.CompilerParams(vmem_limit_bytes=48 << 20),
    )


def in_hbm(operand):
    return pltpu.with_memory_space_constraint(operand, pltpu.HBM)


def shifted(value, axis, shift):
    size = lax.axis_size(axis)
    return lax.ppermute(value, axis, [(i, (i + shift) % size) for i in range(size)])


def local(
    vol_rhs,
    surf_rhs,
    vol_blocks,
    vol_cols,
    coupling,
    trace_map,
    bnd_count,
    surf_inverse,
    near_blocks,
    near_cols,
    far_u,
    far_v,
):
    angles, width = surf_rhs.shape
    vol_count, terms, bs, _ = vol_blocks.shape
    slots = coupling.shape[0]
    nv, nr, nc = (lax.axis_size(a) for a in ("vol", "row", "col"))
    piece = (angles, width)
    product = 2 * angles * bs * bs

    def shape(dims, dtype):
        return jax.ShapeDtypeStruct(dims, dtype)

    tables = (vol_cols.T, trace_map)
    payload_shapes = [shape((2 * angles, width), HALF)] * (nv - 1)
    start_shapes = [shape(piece, F32), shape(piece, HALF), shape(piece, F32)] + payload_shapes
    totals = pltpu.VMEM((nv,) + piece, F32)
    field = pltpu.VMEM((vol_count, angles, bs), HALF)

    kept = (near_blocks, near_cols, far_u, far_v)
    started = call(
        functools.partial(start_kernel, "vol", len(start_shapes), len(kept)),
        "start",
        [SMEM] + [HBM] * (7 + len(kept)),
        start_shapes + [pltpu.VMEM(a.shape, a.dtype) for a in tables + kept],
        product * slots * (terms + 1),
        2 * bs * bs * slots * (terms + 1),
        [
            pltpu.VMEM(piece, HALF),
            pltpu.VMEM(surf_inverse.shape, HALF),
            pltpu.VMEM(vol_rhs.shape, HALF),
            pltpu.VMEM((slots, terms, bs, bs), HALF),
            pltpu.VMEM(coupling.shape, HALF),
            *(pltpu.SMEM(t.shape, jnp.int32) for t in tables),
            totals,
            pltpu.SemaphoreType.DMA((8 + slots + len(kept),)),
        ],
    )(bnd_count, *map(in_hbm, (surf_rhs, surf_inverse, vol_rhs, vol_blocks, coupling) + tables + kept))
    surface, half, own_trace, *payloads = started[: len(start_shapes)]
    kept = started[len(start_shapes) :]
    tables, kept = (*kept[:2], bnd_count), kept[2:]

    (dense,) = call(
        functools.partial(dense_kernel, nv, nr, nc),
        "dense",
        [VMEM, SMEM, VMEM, VMEM],
        [shape((nv * nr * width, nc * width), HALF)],
        product * nv * nr * nc,
        4 * nv * nr * nc * bs * bs,
        [pltpu.VMEM((nv * nr * width, bs), F32)],
    )(*kept)

    for iteration in range(ITERS):
        received = [shifted(payloads[k - 1], "vol", k) for k in range(1, nv)]
        group = jnp.concatenate([half] + [r[:angles] for r in received], axis=0)
        if iteration == 0:
            group, dense = lax.optimization_barrier((group, dense))
        groups = [group] + [shifted(group, "row", k) for k in range(1, nr)]
        last = iteration == ITERS - 1
        if last:
            split = vol_count // 2
            early, residual = call(
                functools.partial(early_kernel, "vol", nv),
                "early_volume",
                [VMEM] * 4 + [SMEM] * 3,
                [shape((angles, split * bs), F32), shape((vol_count, angles, bs), HALF)],
                product * split * terms,
                2 * bs * bs * split * terms,
            )(group, vol_rhs, vol_blocks, coupling, *tables)
            beside = early
        else:
            (total,) = call(
                functools.partial(boundary_kernel, "vol"),
                "boundary",
                [VMEM] * 4 + [SMEM] * 3,
                [shape((nv,) + piece, F32)],
                product * slots * (terms + 2),
                2 * bs * bs * slots * (terms + 1),
                [field],
            )(group, vol_rhs, vol_blocks, coupling, *tables)
            beside = total
        integral, *parts = call(
            functools.partial(integral_kernel, nr, nv),
            "integral",
            [VMEM] * (nr + 1) + [ANY],
            [shape(piece, F32)] + [shape(piece, HALF)] * (nc - 1),
            product * nv * nr * nc,
            2 * nv * nr * nc * width * width,
        )(*groups, dense, beside)
        sums = [shifted(parts[k - 1], "col", k) for k in range(1, nc)]
        if last:
            (volume,) = call(
                late_kernel,
                "late_volume",
                [VMEM] * 3 + [SMEM],
                [shape((angles, vol_count * bs), F32)],
                product * (vol_count - split) * terms,
                2 * bs * bs * (vol_count - split) * terms,
            )(early, residual, vol_blocks, tables[0])
            (surface,) = call(
                functools.partial(last_kernel, nc - 1, nv - 1),
                "last",
                [VMEM] * (5 + nc - 1 + nv - 1),
                [shape(piece, F32)],
                product,
                1 << 17,
            )(surface, surf_rhs, surf_inverse, integral, own_trace, *sums, *received)
        else:
            surface, half, own_trace, *payloads = call(
                functools.partial(step_kernel, nc - 1, nv - 1),
                "step",
                [VMEM] * (6 + nc - 1 + nv - 1),
                [shape(piece, F32), shape(piece, HALF), shape(piece, F32)] + payload_shapes,
                product,
                1 << 17,
            )(surface, surf_rhs, surf_inverse, integral, own_trace, total, *sums, *received)
    return volume, surface


def solution(mesh):
    everywhere = ("vol", "row", "col")
    in_specs = (
        P(None, everywhere),
        P(None, everywhere),
        P(everywhere, None, None, None),
        P(everywhere, None),
        P(everywhere, None, None),
        P(everywhere),
        P(everywhere),
        P(everywhere, None, None),
        P(("vol", "row"), "col", None, None, None),
        P(("vol", "row"), "col", None),
        P("col", None, ("vol", "row")),
        P(("vol", "row"), "col", None, None),
    )
    out_specs = (P(None, everywhere), P(None, everywhere))
    return jax.shard_map(local, mesh=mesh, in_specs=in_specs, out_specs=out_specs, check_vma=False)
```

```python
import functools

import jax
import jax.numpy as jnp
from jax import lax
from jax.experimental import pallas as pl
from jax.experimental.pallas import tpu as pltpu
from jax.sharding import PartitionSpec as P

UNROLL = 16
INTEGRAL_COST = 10**9
STEP_COST = 10**9
F32 = jnp.float32
HALF = jnp.bfloat16


def by_rows(a, b):
    return lax.dot_general(a, b, (((1,), (1,)), ((), ())), preferred_element_type=F32)


def by_cols(a, b):
    return lax.dot_general(a, b, (((1,), (0,)), ((), ())), preferred_element_type=F32)


def block(start, size):
    return pl.ds(pl.multiple_of(start * size, size), size)


def slot_of(index, here, count):
    return lax.rem(index - here + count, count)


def pair_size(rows):
    return 2 if rows % 2 == 0 else 1


def block_row(read, blocks, columns, row):
    terms = blocks.shape[1]
    field = jnp.concatenate([read(columns[n, row]) for n in range(terms)], axis=1)
    inverse = jnp.concatenate([blocks[row, n] for n in range(terms)], axis=1)
    return by_rows(field, inverse)


def add_traces(total, boundary, coupling, trace_map, bnd_count, axis):
    count = total.shape[0]
    bs = coupling.shape[-1]
    subs = total.shape[2] // bs
    here = lax.axis_index(axis)
    for j in range(coupling.shape[0]):
        alive = (j < bnd_count[0]).astype(F32)
        contrib = by_cols(boundary(j), coupling[j]) * alive
        target = trace_map[j]
        slot = slot_of(target // subs, here, count)
        where = (slot, slice(None), block(lax.rem(target, subs), bs))
        total[where] = total[where] + contrib


def residual_blocks(resid, vol_rhs, group, coupling, trace_map, bnd_count, axis, count, stride):
    bs = coupling.shape[-1]
    angles = vol_rhs.shape[0]
    subs = group.shape[1] // bs
    here = lax.axis_index(axis)
    for j in range(coupling.shape[0]):
        alive = (j < bnd_count[0]).astype(F32)
        target = trace_map[j]
        slot = slot_of(here, target // subs, count)
        picked = group[block(slot * stride, angles), block(lax.rem(target, subs), bs)]
        current = by_rows(picked, coupling[j]) * alive
        rhs = vol_rhs[:, j * bs : (j + 1) * bs].astype(F32)
        resid[j] = (rhs - current).astype(HALF)


def send_out(payloads, half, total):
    rows = half.shape[0]
    for k, payload in enumerate(payloads):
        payload[0:rows, :] = half
        payload[rows:, :] = total[k + 1].astype(HALF)


def start_kernel(axis, outs, kept, refs):
    bnd_count, operands, refs = refs[0], refs[1 : 8 + kept], refs[8 + kept :]
    half_out, own_trace, *payloads = refs[:outs]
    copied, refs = refs[outs : outs + kept + 2], refs[outs + kept + 2 :]
    surf_rhs, surf_inverse, vol_rhs, blocks, coupling, columns, trace_map, total, sems = refs
    slots = coupling.shape[0]
    bs = coupling.shape[-1]
    count = iter(range(sems.shape[0]))

    def copy(source, to):
        started = pltpu.make_async_copy(source, to, sems.at[next(count)])
        started.start()
        return started

    tables = [copy(operands[5 + i], t) for i, t in enumerate((columns, trace_map))]
    first = [copy(operands[0], surf_rhs), copy(operands[1], surf_inverse)]
    tables.append(copy(operands[2], vol_rhs))
    rows = [copy(operands[3].at[j], blocks.at[j]) for j in range(slots)]
    last = copy(operands[4], coupling)
    later = [copy(operands[5 + i], t) for i, t in enumerate(copied)]
    total[...] = jnp.zeros_like(total)
    for c in first:
        c.wait()
    for b in range(surf_inverse.shape[0]):
        cols = slice(b * bs, (b + 1) * bs)
        half_out[:, cols] = by_rows(surf_rhs[:, cols], surf_inverse[b]).astype(HALF)
    for c in tables:
        c.wait()
    solved = []
    for j in range(slots):
        rows[j].wait()
        read = lambda col: vol_rhs[:, block(col, bs)]
        solved.append(block_row(read, blocks, columns, j).astype(HALF))
    last.wait()
    add_traces(total, lambda j: solved[j], coupling, trace_map, bnd_count, axis)
    own_trace[...] = total[0]
    send_out(payloads, half_out[...], total)
    for c in later:
        c.wait()


def boundary_kernel(axis, refs):
    (group, vol_rhs, blocks, coupling, columns, trace_map, bnd_count, total, field) = refs
    bs = coupling.shape[-1]
    slots = coupling.shape[0]
    count = total.shape[0]
    for b in range(slots, vol_rhs.shape[1] // bs):
        field[b] = vol_rhs[:, b * bs : (b + 1) * bs]
    residual_blocks(field, vol_rhs, group, coupling, trace_map, bnd_count, axis, count, 1)
    total[...] = jnp.zeros_like(total)

    def boundary(j):
        return block_row(lambda col: field[col], blocks, columns, j).astype(HALF)

    add_traces(total, boundary, coupling, trace_map, bnd_count, axis)


def early_kernel(axis, count, stride, refs):
    (group, vol_rhs, blocks, coupling, columns, trace_map, bnd_count, early, field) = refs
    bs = coupling.shape[-1]
    for b in range(coupling.shape[0], vol_rhs.shape[1] // bs):
        field[b] = vol_rhs[:, b * bs : (b + 1) * bs]
    residual_blocks(field, vol_rhs, group, coupling, trace_map, bnd_count, axis, count, stride)
    for b in range(early.shape[1] // bs):
        early[:, b * bs : (b + 1) * bs] = block_row(lambda col: field[col], blocks, columns, b)


def late_kernel(refs):
    early, field, blocks, columns, volume = refs
    bs = field.shape[-1]
    first = early.shape[1] // bs
    volume[:, : first * bs] = early[...]
    for b in range(first, blocks.shape[0]):
        volume[:, b * bs : (b + 1) * bs] = block_row(lambda col: field[col], blocks, columns, b)


def dense_kernel(vol_size, row_size, col_size, refs):
    near_blocks, near_cols, far_u, far_v, surf_rhs, surf_inverse, dense, *messages, work = refs
    bs = near_blocks.shape[-1]
    rows = near_blocks.shape[0]
    subs = rows // col_size
    pair = pair_size(row_size)
    chips = row_size // pair
    vol, row, col = (lax.axis_index(name) for name in ("vol", "row", "col"))

    def place(number):
        piece = number // subs
        from_row = lax.rem(piece, row_size)
        chip_slot = slot_of(row // pair, from_row // pair, chips)
        pair_slot = slot_of(lax.rem(row, pair), lax.rem(from_row, pair), pair)
        vol_slot = slot_of(vol, piece // row_size, vol_size)
        slot = (chip_slot * pair + pair_slot) * vol_size + vol_slot
        return slot * subs + lax.rem(number, subs)

    total = vol_size * row_size * subs
    part = total * bs // chips
    for k in range(col_size):
        piece = lax.rem(col + k, col_size)
        for sub in range(subs):
            b = piece * subs + sub
            u = far_u[0, :, block(b, bs)]

            def far(number, _):
                v = far_v[0, 0, :, block(number, bs)]
                work[block(place(number), bs), :] = lax.dot_general(
                    v, u, (((0,), (0,)), ((), ())), preferred_element_type=F32
                )
                return _

            lax.fori_loop(0, total, far, 0, unroll=min(total, UNROLL))
            for n in range(near_blocks.shape[2]):
                where = (block(place(near_cols[b, 0, n]), bs), slice(None))
                work[where] = work[where] + near_blocks[b, 0, n].astype(F32).T
            at = (k * subs + sub) * bs
            dense[:, at : at + bs] = work[...].astype(HALF)
            for a in range(chips):
                if a or k:
                    message = messages[a * col_size + k - 1]
                    message[0:part, sub * bs : (sub + 1) * bs] = work[
                        a * part : (a + 1) * part, :
                    ].astype(HALF)
    angles = surf_rhs.shape[0]
    for k in range(1, col_size):
        message = messages[k - 1]
        message[part : part + angles, :] = surf_rhs[...]
        for sub in range(subs):
            at = part + angles + sub * bs
            message[at : at + bs, sub * bs : (sub + 1) * bs] = surf_inverse[sub]


def add_received(total, received):
    for r in received:
        total = total + r[-total.shape[0] :, :].astype(F32)
    return total


def integral_kernel(row_size, vol_size, col_size, refs):
    groups, refs = refs[:row_size], refs[row_size:]
    dense, own_trace, *received, _, parts, message = refs
    angles, width = own_trace.shape
    field = jnp.concatenate(
        [g[k * angles : (k + 1) * angles, :] for g in groups for k in range(vol_size)], axis=1
    )
    part = by_cols(field, dense[...])
    for k in range(col_size):
        rows = slice(k * angles, (k + 1) * angles)
        term = part[:, k * width : (k + 1) * width]
        if k == 0:
            term = term + add_received(own_trace[...], received)
        parts[rows, :] = term
        message[rows, :] = term.astype(HALF)


def step_kernel(col_size, refs):
    parts, surf_rhs, surf_inverse, total, *refs = refs
    neighbours, refs = refs[: col_size - 1], refs[col_size - 1 :]
    messages, refs = refs[: col_size - 1], refs[col_size - 1 :]
    surface, half, next_trace, *payloads = refs
    angles = surf_rhs.shape[0]
    bs = surf_inverse.shape[-1]
    subs = surf_inverse.shape[0]
    for j in range(col_size):
        taken = parts[j * angles : (j + 1) * angles, :]
        for shift, message in enumerate(messages, 1):
            k = (j + shift) % col_size
            taken = taken + message[k * angles : (k + 1) * angles, :].astype(F32)
        source = None if j == 0 else neighbours[col_size - j - 1]
        first = 0 if j == 0 else source.shape[0] - angles - subs * bs
        for sub in range(subs):
            cols = slice(sub * bs, (sub + 1) * bs)
            if j == 0:
                rhs, inverse = surf_rhs[:, cols], surf_inverse[sub]
            else:
                at = first + angles + sub * bs
                rhs, inverse = source[first : first + angles, cols], source[at : at + bs, cols]
            resid = (rhs.astype(F32) - taken[:, cols]).astype(HALF)
            value = by_rows(rhs, inverse) + by_rows(resid, inverse)
            if j == 0:
                surface[:, cols] = value
            half[j * angles : (j + 1) * angles, cols] = value.astype(HALF)
    next_trace[...] = total[0]
    send_out(payloads, half[...], total)


def last_integral_kernel(pair, vol_size, col_size, chips, refs):
    groups, refs = refs[:pair], refs[pair:]
    dense, refs = refs[0], refs[1:]
    blocks, outs = refs[: chips * col_size - 1], refs[chips * col_size - 1 :][-chips:]
    angles, width = outs[0].shape
    part = dense.shape[0] // chips
    total = jnp.zeros((angles, chips * width), F32)
    for b in range(col_size):
        place = (col_size - b) % col_size
        field = []
        for g in groups:
            for k in range(vol_size):
                at = (k * col_size + place) * angles
                field.append(g[at : at + angles, :])
        matrix = []
        for a in range(chips):
            own = a == 0 and b == 0
            source = dense if own else blocks[a * col_size + b - 1]
            matrix.append(source[0:part, 0:width])
        total = total + by_cols(
            jnp.concatenate(field, axis=1), jnp.concatenate(matrix, axis=1)
        )
    for a, out in enumerate(outs):
        out[...] = total[:, a * width : (a + 1) * width].astype(out.dtype)


def last_kernel(sums, refs):
    surface, surf_rhs, surf_inverse, integral, own_trace, *refs = refs
    sums, received, out = refs[:sums], refs[sums:-1], refs[-1]
    bs = surf_inverse.shape[-1]
    taken = add_received(integral[...] + own_trace[...], received)
    for s in sums:
        taken = taken + s[...].astype(F32)
    resid = (surf_rhs[...].astype(F32) - taken).astype(HALF)
    for b in range(surf_inverse.shape[0]):
        cols = slice(b * bs, (b + 1) * bs)
        out[:, cols] = surface[:, cols] + by_rows(resid[:, cols], surf_inverse[b])


VMEM = pl.BlockSpec(memory_space=pltpu.VMEM)
SMEM = pl.BlockSpec(memory_space=pltpu.SMEM)


ANY = pl.BlockSpec(memory_space=pl.ANY)
HBM = pl.BlockSpec(memory_space=pltpu.HBM)


def call(body, name, in_specs, outs, flops, moved, scratch=()):
    def kernel(*refs):
        body(refs)

    return pl.pallas_call(
        kernel,
        name=name,
        out_shape=outs,
        in_specs=in_specs,
        out_specs=[VMEM] * len(outs),
        scratch_shapes=list(scratch),
        cost_estimate=pl.CostEstimate(flops=flops, bytes_accessed=moved, transcendentals=0),
        compiler_params=pltpu.CompilerParams(vmem_limit_bytes=48 << 20),
    )


def in_hbm(operand):
    return pltpu.with_memory_space_constraint(operand, pltpu.HBM)


def shifted(value, axis, shift):
    size = lax.axis_size(axis)
    return lax.ppermute(value, axis, [(i, (i + shift) % size) for i in range(size)])


def shifted_in_plane(value, chip, core=0, col=0):
    rows, cols = lax.axis_size("row"), lax.axis_size("col")
    pair = pair_size(rows)
    chips = rows // pair
    pairs = []
    for r in range(rows):
        to = (r // pair + chip) % chips * pair + (r % pair + core) % pair
        pairs += [(r * cols + c, to * cols + (c + col) % cols) for c in range(cols)]
    return lax.ppermute(value, ("row", "col"), pairs)


def local(
    vol_rhs,
    surf_rhs,
    vol_blocks,
    vol_cols,
    coupling,
    trace_map,
    bnd_count,
    surf_inverse,
    near_blocks,
    near_cols,
    far_u,
    far_v,
):
    angles, width = surf_rhs.shape
    vol_count, terms, bs, _ = vol_blocks.shape
    slots = coupling.shape[0]
    nv, nr, nc = (lax.axis_size(a) for a in ("vol", "row", "col"))
    piece = (angles, width)
    product = 2 * angles * bs * bs

    def shape(dims, dtype):
        return jax.ShapeDtypeStruct(dims, dtype)

    tables = (vol_cols.T, trace_map)
    payload_shapes = [shape((2 * angles, width), HALF)] * (nv - 1)
    start_shapes = [shape(piece, HALF), shape(piece, F32)] + payload_shapes
    totals = pltpu.VMEM((nv,) + piece, F32)
    field = pltpu.VMEM((vol_count, angles, bs), HALF)

    kept = (near_blocks, near_cols, far_u, far_v, surf_rhs, surf_inverse)
    started = call(
        functools.partial(start_kernel, "vol", len(start_shapes), len(kept)),
        "start",
        [SMEM] + [HBM] * (7 + len(kept)),
        start_shapes + [pltpu.VMEM(a.shape, a.dtype) for a in tables + kept],
        product * slots * (terms + 1),
        2 * bs * bs * slots * (terms + 1),
        [
            pltpu.VMEM(piece, HALF),
            pltpu.VMEM(surf_inverse.shape, HALF),
            pltpu.VMEM(vol_rhs.shape, HALF),
            pltpu.VMEM((slots, terms, bs, bs), HALF),
            pltpu.VMEM(coupling.shape, HALF),
            *(pltpu.SMEM(t.shape, jnp.int32) for t in tables),
            totals,
            pltpu.SemaphoreType.DMA((8 + slots + len(kept),)),
        ],
    )(bnd_count, *map(in_hbm, (surf_rhs, surf_inverse, vol_rhs, vol_blocks, coupling) + tables + kept))
    half, own_trace, *payloads = started[: len(start_shapes)]
    kept = started[len(start_shapes) :]
    tables, kept = (*kept[:2], bnd_count), kept[2:]

    pair = pair_size(nr)
    chips = nr // pair
    part = nv * pair * width
    sizes = [
        part + (angles + surf_inverse.shape[0] * bs if a == 0 else 0)
        for a in range(chips)
        for b in range(nc)
    ]
    dense, *messages = call(
        functools.partial(dense_kernel, nv, nr, nc),
        "dense",
        [VMEM, SMEM] + [VMEM] * 4,
        [shape((nv * nr * width, nc * width), HALF)]
        + [shape((size, width), HALF) for size in sizes[1:]],
        product * nv * nr * nc,
        4 * nv * nr * nc * bs * bs,
        [pltpu.VMEM((nv * nr * width, bs), F32)],
    )(*kept)

    received = [shifted(payloads[k - 1], "vol", k) for k in range(1, nv)]
    blocks = [
        shifted_in_plane(messages[i - 1], chip=-(i // nc), col=i % nc) for i in range(1, nc)
    ]
    group = jnp.concatenate([half] + [r[:angles] for r in received], axis=0)
    group, dense = lax.optimization_barrier((group, dense))
    groups = [group] + [
        shifted_in_plane(group, chip=i // pair, core=i % pair) for i in range(1, nr)
    ]
    (total,) = call(
        functools.partial(boundary_kernel, "vol"),
        "boundary",
        [VMEM] * 4 + [SMEM] * 3,
        [shape((nv,) + piece, F32)],
        product * slots * (terms + 2),
        2 * bs * bs * slots * (terms + 1),
        [field],
    )(group, vol_rhs, vol_blocks, coupling, *tables)
    ahead = [
        shifted_in_plane(messages[i - 1], chip=-(i // nc), col=0) for i in range(nc, nc * chips, nc)
    ]
    parts, message = call(
        functools.partial(integral_kernel, nr, nv, nc),
        "integral",
        [VMEM] * (nr + nv + 1) + [ANY],
        [shape((nc * angles, width), F32), shape((nc * angles, width), HALF)],
        INTEGRAL_COST,
        2 * nv * nr * nc * width * width,
    )(*groups, dense, own_trace, *received, total)
    sums = [shifted(message, "col", k) for k in range(1, nc)]
    parts, *later = lax.optimization_barrier(
        (parts, *(messages[i - 1] for i in range(nc, nc * chips) if i % nc))
    )
    later = iter(later)
    after = {
        i: shifted_in_plane(next(later), chip=-(i // nc), col=i % nc)
        for i in range(nc, nc * chips)
        if i % nc
    }
    surface, half, own_trace, *payloads = call(
        functools.partial(step_kernel, nc),
        "step",
        [VMEM] * (4 + 2 * (nc - 1)),
        [shape(piece, F32), shape((nc * angles, width), HALF), shape(piece, F32)]
        + [shape(((nc + 1) * angles, width), HALF)] * (nv - 1),
        STEP_COST,
        nc << 17,
    )(parts, surf_rhs, surf_inverse, total, *blocks, *sums)

    received = [shifted(payloads[k - 1], "vol", k) for k in range(1, nv)]
    received, ahead = lax.optimization_barrier((received, ahead))
    group = jnp.concatenate([half] + [r[: nc * angles] for r in received], axis=0)
    group, after = lax.optimization_barrier((group, after))
    blocks += [
        after[i] if i % nc else ahead[i // nc - 1] for i in range(nc, nc * chips)
    ]
    groups = [group] + [shifted_in_plane(group, chip=0, core=k) for k in range(1, pair)]
    split = vol_count // 2
    early, residual = call(
        functools.partial(early_kernel, "vol", nv, nc),
        "early_volume",
        [VMEM] * 4 + [SMEM] * 3,
        [shape((angles, split * bs), F32), shape((vol_count, angles, bs), HALF)],
        product * split * terms,
        2 * bs * bs * split * terms,
    )(group, vol_rhs, vol_blocks, coupling, *tables)
    integral, *parts = call(
        functools.partial(last_integral_kernel, pair, nv, nc, chips),
        "last_integral",
        [VMEM] * (pair + chips * nc) + [ANY],
        [shape(piece, F32)] + [shape(piece, HALF)] * (chips - 1),
        product * nv * nr * nc,
        2 * nv * nr * nc * width * width,
    )(*groups, dense, *blocks, early)
    sums = [shifted_in_plane(parts[a - 1], chip=a) for a in range(1, chips)]
    (volume,) = call(
        late_kernel,
        "late_volume",
        [VMEM] * 3 + [SMEM],
        [shape((angles, vol_count * bs), F32)],
        product * (vol_count - split) * terms,
        2 * bs * bs * (vol_count - split) * terms,
    )(early, residual, vol_blocks, tables[0])
    (surface,) = call(
        functools.partial(last_kernel, chips - 1),
        "last",
        [VMEM] * (5 + chips - 1 + nv - 1),
        [shape(piece, F32)],
        product,
        1 << 17,
    )(surface, surf_rhs, surf_inverse, integral, own_trace, *sums, *received)
    return volume, surface


def solution(mesh):
    everywhere = ("vol", "row", "col")
    in_specs = (
        P(None, everywhere),
        P(None, everywhere),
        P(everywhere, None, None, None),
        P(everywhere, None),
        P(everywhere, None, None),
        P(everywhere),
        P(everywhere),
        P(everywhere, None, None),
        P(("vol", "row"), "col", None, None, None),
        P(("vol", "row"), "col", None),
        P("col", None, ("vol", "row")),
        P(("vol", "row"), "col", None, None),
    )
    out_specs = (P(None, everywhere), P(None, everywhere))
    return jax.shard_map(local, mesh=mesh, in_specs=in_specs, out_specs=out_specs, check_vma=False)
```

```python
import functools

import jax
import jax.numpy as jnp
from jax import lax
from jax.experimental import pallas as pl
from jax.experimental.pallas import tpu as pltpu
from jax.sharding import PartitionSpec as P

UNROLL = 16
INTEGRAL_COST = 10**9
STEP_COST = 10**9
F32 = jnp.float32
HALF = jnp.bfloat16


def by_rows(a, b):
    return lax.dot_general(a, b, (((1,), (1,)), ((), ())), preferred_element_type=F32)


def by_cols(a, b):
    return lax.dot_general(a, b, (((1,), (0,)), ((), ())), preferred_element_type=F32)


def block(start, size):
    return pl.ds(pl.multiple_of(start * size, size), size)


def slot_of(index, here, count):
    return lax.rem(index - here + count, count)


def pair_size(rows):
    return 2 if rows % 2 == 0 else 1


def block_row(read, blocks, columns, row):
    terms = blocks.shape[1]
    field = jnp.concatenate([read(columns[n, row]) for n in range(terms)], axis=1)
    inverse = jnp.concatenate([blocks[row, n] for n in range(terms)], axis=1)
    return by_rows(field, inverse)


def add_traces(total, boundary, coupling, trace_map, bnd_count, axis):
    count = total.shape[0]
    bs = coupling.shape[-1]
    subs = total.shape[2] // bs
    here = lax.axis_index(axis)
    for j in range(coupling.shape[0]):
        alive = (j < bnd_count[0]).astype(F32)
        contrib = by_cols(boundary(j), coupling[j]) * alive
        target = trace_map[j]
        slot = slot_of(target // subs, here, count)
        where = (slot, slice(None), block(lax.rem(target, subs), bs))
        total[where] = total[where] + contrib


def residual_blocks(resid, vol_rhs, group, coupling, trace_map, bnd_count, axis, count, stride):
    bs = coupling.shape[-1]
    angles = vol_rhs.shape[0]
    subs = group.shape[1] // bs
    here = lax.axis_index(axis)
    for j in range(coupling.shape[0]):
        alive = (j < bnd_count[0]).astype(F32)
        target = trace_map[j]
        slot = slot_of(here, target // subs, count)
        picked = group[block(slot * stride, angles), block(lax.rem(target, subs), bs)]
        current = by_rows(picked, coupling[j]) * alive
        rhs = vol_rhs[:, j * bs : (j + 1) * bs].astype(F32)
        resid[j] = (rhs - current).astype(HALF)


def send_out(payloads, half, total):
    rows = half.shape[0]
    for k, payload in enumerate(payloads):
        payload[0:rows, :] = half
        payload[rows:, :] = total[k + 1].astype(HALF)


def start_kernel(axis, outs, kept, refs):
    bnd_count, operands, refs = refs[0], refs[1 : 8 + kept], refs[8 + kept :]
    half_out, own_trace, *payloads = refs[:outs]
    loaded, copied, refs = refs[outs : outs + 5], refs[outs + 5 : outs + 7 + kept], refs[outs + 7 + kept :]
    surf_rhs, surf_inverse, vol_rhs, blocks, coupling = loaded
    columns, trace_map, total, sems = refs
    slots = coupling.shape[0]
    bs = coupling.shape[-1]
    count = iter(range(sems.shape[0]))

    def copy(source, to):
        started = pltpu.make_async_copy(source, to, sems.at[next(count)])
        started.start()
        return started

    tables = [copy(operands[5 + i], t) for i, t in enumerate((columns, trace_map))]
    first = [copy(operands[0], surf_rhs), copy(operands[1], surf_inverse)]
    tables.append(copy(operands[2], vol_rhs))
    rows = [copy(operands[3].at[j], blocks.at[j]) for j in range(slots)]
    last = copy(operands[4], coupling)
    later = [copy(operands[5 + i], t) for i, t in enumerate(copied)]
    total[...] = jnp.zeros_like(total)
    for c in first:
        c.wait()
    for b in range(surf_inverse.shape[0]):
        cols = slice(b * bs, (b + 1) * bs)
        half_out[:, cols] = by_rows(surf_rhs[:, cols], surf_inverse[b]).astype(HALF)
    for c in tables:
        c.wait()
    solved = []
    for j in range(slots):
        rows[j].wait()
        read = lambda col: vol_rhs[:, block(col, bs)]
        solved.append(block_row(read, blocks, columns, j).astype(HALF))
    last.wait()
    add_traces(total, lambda j: solved[j], coupling, trace_map, bnd_count, axis)
    own_trace[...] = total[0]
    send_out(payloads, half_out[...], total)
    for c in later:
        c.wait()


def boundary_kernel(axis, refs):
    group, vol_rhs, blocks, coupling, *tables, bnd_count, total, field, columns, trace_map, sems = refs
    copies = to_scalars(tables, (columns, trace_map), sems)
    bs = coupling.shape[-1]
    slots = coupling.shape[0]
    count = total.shape[0]
    for b in range(slots, vol_rhs.shape[1] // bs):
        field[b] = vol_rhs[:, b * bs : (b + 1) * bs]
    total[...] = jnp.zeros_like(total)
    for c in copies:
        c.wait()
    residual_blocks(field, vol_rhs, group, coupling, trace_map, bnd_count, axis, count, 1)

    def boundary(j):
        return block_row(lambda col: field[col], blocks, columns, j).astype(HALF)

    add_traces(total, boundary, coupling, trace_map, bnd_count, axis)


def early_kernel(axis, count, stride, refs):
    group, vol_rhs, blocks, coupling, *tables, bnd_count, early, field, columns, trace_map, sems = refs
    copies = to_scalars(tables, (columns, trace_map), sems)
    bs = coupling.shape[-1]
    for b in range(coupling.shape[0], vol_rhs.shape[1] // bs):
        field[b] = vol_rhs[:, b * bs : (b + 1) * bs]
    for c in copies:
        c.wait()
    residual_blocks(field, vol_rhs, group, coupling, trace_map, bnd_count, axis, count, stride)
    for b in range(early.shape[1] // bs):
        early[:, b * bs : (b + 1) * bs] = block_row(lambda col: field[col], blocks, columns, b)


def late_kernel(refs):
    early, field, blocks, table, volume, columns, sems = refs
    (copy,) = to_scalars([table], [columns], sems)
    bs = field.shape[-1]
    first = early.shape[1] // bs
    volume[:, : first * bs] = early[...]
    copy.wait()
    for b in range(first, blocks.shape[0]):
        volume[:, b * bs : (b + 1) * bs] = block_row(lambda col: field[col], blocks, columns, b)


def dense_kernel(vol_size, row_size, col_size, refs):
    near_blocks, table, far_u, far_v, surf_rhs, surf_inverse, dense, *messages, work, near_cols, sems = refs
    (copy,) = to_scalars([table], [near_cols], sems)
    bs = near_blocks.shape[-1]
    rows = near_blocks.shape[0]
    subs = rows // col_size
    pair = pair_size(row_size)
    chips = row_size // pair
    vol, row, col = (lax.axis_index(name) for name in ("vol", "row", "col"))

    def place(number):
        piece = number // subs
        from_row = lax.rem(piece, row_size)
        chip_slot = slot_of(row // pair, from_row // pair, chips)
        pair_slot = slot_of(lax.rem(row, pair), lax.rem(from_row, pair), pair)
        vol_slot = slot_of(vol, piece // row_size, vol_size)
        slot = (chip_slot * pair + pair_slot) * vol_size + vol_slot
        return slot * subs + lax.rem(number, subs)

    total = vol_size * row_size * subs
    part = total * bs // chips
    for k in range(col_size):
        piece = lax.rem(col + k, col_size)
        for sub in range(subs):
            b = piece * subs + sub
            u = far_u[0, :, block(b, bs)]

            def far(number, _):
                v = far_v[0, 0, :, block(number, bs)]
                work[block(place(number), bs), :] = lax.dot_general(
                    v, u, (((0,), (0,)), ((), ())), preferred_element_type=F32
                )
                return _

            lax.fori_loop(0, total, far, 0, unroll=min(total, UNROLL))
            if k == 0 and sub == 0:
                copy.wait()
            for n in range(near_blocks.shape[2]):
                where = (block(place(near_cols[b, 0, n]), bs), slice(None))
                work[where] = work[where] + near_blocks[b, 0, n].astype(F32).T
            at = (k * subs + sub) * bs
            dense[:, at : at + bs] = work[...].astype(HALF)
            for a in range(chips):
                if a or k:
                    message = messages[a * col_size + k - 1]
                    message[0:part, sub * bs : (sub + 1) * bs] = work[
                        a * part : (a + 1) * part, :
                    ].astype(HALF)
    angles = surf_rhs.shape[0]
    for k in range(1, col_size):
        message = messages[k - 1]
        message[part : part + angles, :] = surf_rhs[...]
        for sub in range(subs):
            at = part + angles + sub * bs
            message[at : at + bs, sub * bs : (sub + 1) * bs] = surf_inverse[sub]


def to_scalars(tables, held, sems):
    copies = [
        pltpu.make_async_copy(table, to, sems.at[i])
        for i, (table, to) in enumerate(zip(tables, held, strict=True))
    ]
    for c in copies:
        c.start()
    return copies


def add_received(total, received):
    for r in received:
        total = total + r[-total.shape[0] :, :].astype(F32)
    return total


def integral_kernel(row_size, vol_size, col_size, refs):
    groups, refs = refs[row_size - 1 :: -1], refs[row_size:]
    dense, own_trace, *received, _, parts, message = refs
    angles, width = own_trace.shape
    field = jnp.concatenate(
        [g[k * angles : (k + 1) * angles, :] for g in groups for k in range(vol_size)], axis=1
    )
    part = by_cols(field, dense[...])
    for k in range(col_size):
        rows = slice(k * angles, (k + 1) * angles)
        term = part[:, k * width : (k + 1) * width]
        if k == 0:
            term = term + add_received(own_trace[...], received)
        parts[rows, :] = term
        message[rows, :] = term.astype(HALF)


def step_kernel(col_size, refs):
    parts, surf_rhs, surf_inverse, total, *refs = refs
    neighbours, refs = refs[: col_size - 1], refs[col_size - 1 :]
    messages, refs = refs[: col_size - 1], refs[col_size - 1 :]
    surface, half, next_trace, *payloads = refs
    angles = surf_rhs.shape[0]
    bs = surf_inverse.shape[-1]
    subs = surf_inverse.shape[0]
    for j in range(col_size):
        taken = parts[j * angles : (j + 1) * angles, :]
        for shift, message in enumerate(messages, 1):
            k = (j + shift) % col_size
            taken = taken + message[k * angles : (k + 1) * angles, :].astype(F32)
        source = None if j == 0 else neighbours[col_size - j - 1]
        first = 0 if j == 0 else source.shape[0] - angles - subs * bs
        for sub in range(subs):
            cols = slice(sub * bs, (sub + 1) * bs)
            if j == 0:
                rhs, inverse = surf_rhs[:, cols], surf_inverse[sub]
            else:
                at = first + angles + sub * bs
                rhs, inverse = source[first : first + angles, cols], source[at : at + bs, cols]
            resid = (rhs.astype(F32) - taken[:, cols]).astype(HALF)
            value = by_rows(rhs, inverse) + by_rows(resid, inverse)
            if j == 0:
                surface[:, cols] = value
            half[j * angles : (j + 1) * angles, cols] = value.astype(HALF)
    next_trace[...] = total[0]
    send_out(payloads, half[...], total)


def last_integral_kernel(pair, vol_size, col_size, chips, refs):
    groups, refs = refs[:pair], refs[pair:]
    dense, refs = refs[0], refs[1:]
    blocks, outs = refs[: chips * col_size - 1], refs[chips * col_size - 1 :][-chips:]
    angles, width = outs[0].shape
    part = dense.shape[0] // chips
    total = jnp.zeros((angles, chips * width), F32)
    for b in range(col_size):
        place = (col_size - b) % col_size
        field = []
        for g in groups:
            for k in range(vol_size):
                at = (k * col_size + place) * angles
                field.append(g[at : at + angles, :])
        matrix = []
        for a in range(chips):
            own = a == 0 and b == 0
            source = dense if own else blocks[a * col_size + b - 1]
            matrix.append(source[0:part, 0:width])
        total = total + by_cols(
            jnp.concatenate(field, axis=1), jnp.concatenate(matrix, axis=1)
        )
    for a, out in enumerate(outs):
        out[...] = total[:, a * width : (a + 1) * width].astype(out.dtype)


def last_kernel(sums, refs):
    surface, surf_rhs, surf_inverse, integral, own_trace, *refs = refs
    sums, received, out = refs[:sums], refs[sums:-1], refs[-1]
    bs = surf_inverse.shape[-1]
    taken = add_received(integral[...] + own_trace[...], received)
    for s in sums:
        taken = taken + s[...].astype(F32)
    resid = (surf_rhs[...].astype(F32) - taken).astype(HALF)
    for b in range(surf_inverse.shape[0]):
        cols = slice(b * bs, (b + 1) * bs)
        out[:, cols] = surface[:, cols] + by_rows(resid[:, cols], surf_inverse[b])


VMEM = pl.BlockSpec(memory_space=pltpu.VMEM)
SMEM = pl.BlockSpec(memory_space=pltpu.SMEM)


ANY = pl.BlockSpec(memory_space=pl.ANY)
HBM = pl.BlockSpec(memory_space=pltpu.HBM)


def call(body, name, in_specs, outs, flops, moved, scratch=()):
    def kernel(*refs):
        body(refs)

    return pl.pallas_call(
        kernel,
        name=name,
        out_shape=outs,
        in_specs=in_specs,
        out_specs=[VMEM] * len(outs),
        scratch_shapes=list(scratch),
        cost_estimate=pl.CostEstimate(flops=flops, bytes_accessed=moved, transcendentals=0),
        compiler_params=pltpu.CompilerParams(vmem_limit_bytes=48 << 20),
    )


def in_hbm(operand):
    return pltpu.with_memory_space_constraint(operand, pltpu.HBM)


def shifted(value, axis, shift):
    size = lax.axis_size(axis)
    return lax.ppermute(value, axis, [(i, (i + shift) % size) for i in range(size)])


def shifted_in_plane(value, chip, core=0, col=0):
    rows, cols = lax.axis_size("row"), lax.axis_size("col")
    pair = pair_size(rows)
    chips = rows // pair
    pairs = []
    for r in range(rows):
        to = (r // pair + chip) % chips * pair + (r % pair + core) % pair
        pairs += [(r * cols + c, to * cols + (c + col) % cols) for c in range(cols)]
    return lax.ppermute(value, ("row", "col"), pairs)


def local(
    vol_rhs,
    surf_rhs,
    vol_blocks,
    vol_cols,
    coupling,
    trace_map,
    bnd_count,
    surf_inverse,
    near_blocks,
    near_cols,
    far_u,
    far_v,
):
    angles, width = surf_rhs.shape
    vol_count, terms, bs, _ = vol_blocks.shape
    slots = coupling.shape[0]
    nv, nr, nc = (lax.axis_size(a) for a in ("vol", "row", "col"))
    piece = (angles, width)
    product = 2 * angles * bs * bs

    def shape(dims, dtype):
        return jax.ShapeDtypeStruct(dims, dtype)

    tables = (vol_cols.T, trace_map)
    payload_shapes = [shape((2 * angles, width), HALF)] * (nv - 1)
    start_shapes = [shape(piece, HALF), shape(piece, F32)] + payload_shapes
    totals = pltpu.VMEM((nv,) + piece, F32)
    field = pltpu.VMEM((vol_count, angles, bs), HALF)
    scalars = [pltpu.SMEM(t.shape, jnp.int32) for t in tables] + [pltpu.SemaphoreType.DMA((2,))]

    kept = (near_blocks, near_cols, far_u, far_v)
    loaded = (surf_rhs, surf_inverse, vol_rhs, jax.ShapeDtypeStruct((slots, terms, bs, bs), HALF), coupling)
    started = call(
        functools.partial(start_kernel, "vol", len(start_shapes), len(kept)),
        "start",
        [SMEM] + [HBM] * (7 + len(kept)),
        start_shapes + [pltpu.VMEM(a.shape, a.dtype) for a in loaded + tables + kept],
        product * slots * (terms + 1),
        2 * bs * bs * slots * (terms + 1),
        [
            *(pltpu.SMEM(t.shape, jnp.int32) for t in tables),
            totals,
            pltpu.SemaphoreType.DMA((8 + slots + len(kept),)),
        ],
    )(bnd_count, *map(in_hbm, (surf_rhs, surf_inverse, vol_rhs, vol_blocks, coupling) + tables + kept))
    half, own_trace, *payloads = started[: len(start_shapes)]
    surf_rhs, surf_inverse, vol_rhs, boundary_blocks, coupling, *kept = started[len(start_shapes) :]
    tables, kept = (*kept[:2], bnd_count), (*kept[2:], surf_rhs, surf_inverse)

    pair = pair_size(nr)
    chips = nr // pair
    part = nv * pair * width
    sizes = [
        part + (angles + surf_inverse.shape[0] * bs if a == 0 else 0)
        for a in range(chips)
        for b in range(nc)
    ]
    dense, *messages = call(
        functools.partial(dense_kernel, nv, nr, nc),
        "dense",
        [VMEM] * 6,
        [shape((nv * nr * width, nc * width), HALF)]
        + [shape((size, width), HALF) for size in sizes[1:]],
        product * nv * nr * nc,
        4 * nv * nr * nc * bs * bs,
        [
            pltpu.VMEM((nv * nr * width, bs), F32),
            pltpu.SMEM(near_cols.shape, jnp.int32),
            pltpu.SemaphoreType.DMA((1,)),
        ],
    )(*kept)

    received = [shifted(payloads[k - 1], "vol", k) for k in range(1, nv)]
    blocks = [
        shifted_in_plane(messages[i - 1], chip=-(i // nc), col=i % nc) for i in range(1, nc)
    ]
    group = jnp.concatenate([half] + [r[:angles] for r in received], axis=0)
    group, dense = lax.optimization_barrier((group, dense))
    groups = [group] + [
        shifted_in_plane(group, chip=i // pair, core=i % pair) for i in range(1, nr)
    ]
    (total,) = call(
        functools.partial(boundary_kernel, "vol"),
        "boundary",
        [VMEM] * 6 + [SMEM],
        [shape((nv,) + piece, F32)],
        product * slots * (terms + 2),
        2 * bs * bs * slots * (terms + 1),
        [field] + scalars,
    )(group, vol_rhs, boundary_blocks, coupling, *tables)
    ahead = [
        shifted_in_plane(messages[i - 1], chip=-(i // nc), col=0) for i in range(nc, nc * chips, nc)
    ]
    parts, message = call(
        functools.partial(integral_kernel, nr, nv, nc),
        "integral",
        [VMEM] * (nr + nv + 1) + [ANY],
        [shape((nc * angles, width), F32), shape((nc * angles, width), HALF)],
        INTEGRAL_COST,
        2 * nv * nr * nc * width * width,
    )(*groups[::-1], dense, own_trace, *received, total)
    sums = [shifted(message, "col", k) for k in range(1, nc)]
    parts, vol_blocks, *later = lax.optimization_barrier(
        (parts, vol_blocks, *(messages[i - 1] for i in range(nc, nc * chips) if i % nc))
    )
    later = iter(later)
    after = {
        i: shifted_in_plane(next(later), chip=-(i // nc), col=i % nc)
        for i in range(nc, nc * chips)
        if i % nc
    }
    surface, half, own_trace, *payloads = call(
        functools.partial(step_kernel, nc),
        "step",
        [VMEM] * (4 + 2 * (nc - 1)),
        [shape(piece, F32), shape((nc * angles, width), HALF), shape(piece, F32)]
        + [shape(((nc + 1) * angles, width), HALF)] * (nv - 1),
        STEP_COST,
        nc << 17,
    )(parts, surf_rhs, surf_inverse, total, *blocks, *sums)

    received = [shifted(payloads[k - 1], "vol", k) for k in range(1, nv)]
    received, ahead = lax.optimization_barrier((received[1:] + received[:1], ahead))
    received = received[-1:] + received[:-1]
    group = jnp.concatenate([half] + [r[: nc * angles] for r in received], axis=0)
    group, after = lax.optimization_barrier((group, after))
    blocks += [
        after[i] if i % nc else ahead[i // nc - 1] for i in range(nc, nc * chips)
    ]
    groups = [group] + [shifted_in_plane(group, chip=0, core=k) for k in range(1, pair)]
    split = vol_count // 3
    early, residual = call(
        functools.partial(early_kernel, "vol", nv, nc),
        "early_volume",
        [VMEM] * 6 + [SMEM],
        [shape((angles, split * bs), F32), shape((vol_count, angles, bs), HALF)],
        product * split * terms,
        2 * bs * bs * split * terms,
        scalars,
    )(group, vol_rhs, vol_blocks, coupling, *tables)
    integral, *parts = call(
        functools.partial(last_integral_kernel, pair, nv, nc, chips),
        "last_integral",
        [VMEM] * (pair + chips * nc) + [ANY],
        [shape(piece, F32)] + [shape(piece, HALF)] * (chips - 1),
        product * nv * nr * nc,
        2 * nv * nr * nc * width * width,
    )(*groups, dense, *blocks, early)
    sums = [shifted_in_plane(parts[a - 1], chip=a) for a in range(1, chips)]
    (volume,) = call(
        late_kernel,
        "late_volume",
        [VMEM] * 4,
        [shape((angles, vol_count * bs), F32)],
        product * (vol_count - split) * terms,
        2 * bs * bs * (vol_count - split) * terms,
        [scalars[0], pltpu.SemaphoreType.DMA((1,))],
    )(early, residual, vol_blocks, tables[0])
    (surface,) = call(
        functools.partial(last_kernel, chips - 1),
        "last",
        [VMEM] * (5 + chips - 1 + nv - 1),
        [shape(piece, F32)],
        product,
        1 << 17,
    )(surface, surf_rhs, surf_inverse, integral, own_trace, *sums, *received)
    return volume, surface


def solution(mesh):
    everywhere = ("vol", "row", "col")
    in_specs = (
        P(None, everywhere),
        P(None, everywhere),
        P(everywhere, None, None, None),
        P(everywhere, None),
        P(everywhere, None, None),
        P(everywhere),
        P(everywhere),
        P(everywhere, None, None),
        P(("vol", "row"), "col", None, None, None),
        P(("vol", "row"), "col", None),
        P("col", None, ("vol", "row")),
        P(("vol", "row"), "col", None, None),
    )
    out_specs = (P(None, everywhere), P(None, everywhere))
    return jax.shard_map(local, mesh=mesh, in_specs=in_specs, out_specs=out_specs, check_vma=False)
```

```python
import functools

import jax
import jax.numpy as jnp
from jax import lax
from jax.experimental import pallas as pl
from jax.experimental.pallas import tpu as pltpu
from jax.sharding import PartitionSpec as P

UNROLL = 16
INTEGRAL_COST = 10**9
STEP_COST = 10**9
F32 = jnp.float32
HALF = jnp.bfloat16


def by_rows(a, b):
    return lax.dot_general(a, b, (((1,), (1,)), ((), ())), preferred_element_type=F32)


def by_cols(a, b):
    return lax.dot_general(a, b, (((1,), (0,)), ((), ())), preferred_element_type=F32)


def block(start, size):
    return pl.ds(pl.multiple_of(start * size, size), size)


def slot_of(index, here, count):
    return lax.rem(index - here + count, count)


def pair_size(rows):
    return 2 if rows % 2 == 0 else 1


def block_row(read, blocks, columns, row):
    terms = blocks.shape[1]
    field = jnp.concatenate([read(columns[n, row]) for n in range(terms)], axis=1)
    inverse = jnp.concatenate([blocks[row, n] for n in range(terms)], axis=1)
    return by_rows(field, inverse)


def add_traces(total, boundary, coupling, trace_map, bnd_count, axis):
    count = total.shape[0]
    bs = coupling.shape[-1]
    subs = total.shape[2] // bs
    here = lax.axis_index(axis)
    for j in range(coupling.shape[0]):
        alive = (j < bnd_count[0]).astype(F32)
        contrib = by_cols(boundary(j), coupling[j]) * alive
        target = trace_map[j]
        slot = slot_of(target // subs, here, count)
        where = (slot, slice(None), block(lax.rem(target, subs), bs))
        total[where] = total[where] + contrib


def residual_blocks(resid, vol_rhs, group, coupling, trace_map, bnd_count, axis, count, stride):
    bs = coupling.shape[-1]
    angles = vol_rhs.shape[0]
    subs = group.shape[1] // bs
    here = lax.axis_index(axis)
    for j in range(coupling.shape[0]):
        alive = (j < bnd_count[0]).astype(F32)
        target = trace_map[j]
        slot = slot_of(here, target // subs, count)
        picked = group[block(slot * stride, angles), block(lax.rem(target, subs), bs)]
        current = by_rows(picked, coupling[j]) * alive
        rhs = vol_rhs[:, j * bs : (j + 1) * bs].astype(F32)
        resid[j] = (rhs - current).astype(HALF)


def send_out(payloads, half, total):
    rows = half.shape[0]
    for k, payload in enumerate(payloads):
        payload[0:rows, :] = half
        payload[rows:, :] = total[k + 1].astype(HALF)


def start_kernel(axis, outs, kept, refs):
    bnd_count, operands, refs = refs[0], refs[1 : 8 + kept], refs[8 + kept :]
    half_out, own_trace, *payloads = refs[:outs]
    loaded, copied, refs = refs[outs : outs + 5], refs[outs + 5 : outs + 7 + kept], refs[outs + 7 + kept :]
    surf_rhs, surf_inverse, vol_rhs, blocks, coupling = loaded
    columns, trace_map, total, sems = refs
    slots = coupling.shape[0]
    bs = coupling.shape[-1]
    count = iter(range(sems.shape[0]))

    def copy(source, to):
        started = pltpu.make_async_copy(source, to, sems.at[next(count)])
        started.start()
        return started

    tables = [copy(operands[5 + i], t) for i, t in enumerate((columns, trace_map))]
    first = [copy(operands[0], surf_rhs), copy(operands[1], surf_inverse)]
    tables.append(copy(operands[2], vol_rhs))
    rows = [copy(operands[3].at[j], blocks.at[j]) for j in range(slots)]
    last = copy(operands[4], coupling)
    later = [copy(operands[5 + i], t) for i, t in enumerate(copied)]
    total[...] = jnp.zeros_like(total)
    for c in first:
        c.wait()
    for b in range(surf_inverse.shape[0]):
        cols = slice(b * bs, (b + 1) * bs)
        half_out[:, cols] = by_rows(surf_rhs[:, cols], surf_inverse[b]).astype(HALF)
    for c in tables:
        c.wait()
    solved = []
    for j in range(slots):
        rows[j].wait()
        read = lambda col: vol_rhs[:, block(col, bs)]
        solved.append(block_row(read, blocks, columns, j).astype(HALF))
    last.wait()
    add_traces(total, lambda j: solved[j], coupling, trace_map, bnd_count, axis)
    own_trace[...] = total[0]
    send_out(payloads, half_out[...], total)
    for c in later:
        c.wait()


def boundary_kernel(axis, refs):
    group, vol_rhs, blocks, coupling, *tables, bnd_count, total, field, columns, trace_map, sems = refs
    copies = to_scalars(tables, (columns, trace_map), sems)
    bs = coupling.shape[-1]
    slots = coupling.shape[0]
    count = total.shape[0]
    for b in range(slots, vol_rhs.shape[1] // bs):
        field[b] = vol_rhs[:, b * bs : (b + 1) * bs]
    total[...] = jnp.zeros_like(total)
    for c in copies:
        c.wait()
    residual_blocks(field, vol_rhs, group, coupling, trace_map, bnd_count, axis, count, 1)

    def boundary(j):
        return block_row(lambda col: field[col], blocks, columns, j).astype(HALF)

    add_traces(total, boundary, coupling, trace_map, bnd_count, axis)


def early_kernel(axis, count, stride, refs):
    group, vol_rhs, blocks, coupling, *tables, bnd_count, early, field, columns, trace_map, sems = refs
    copies = to_scalars(tables, (columns, trace_map), sems)
    bs = coupling.shape[-1]
    for b in range(coupling.shape[0], vol_rhs.shape[1] // bs):
        field[b] = vol_rhs[:, b * bs : (b + 1) * bs]
    for c in copies:
        c.wait()
    residual_blocks(field, vol_rhs, group, coupling, trace_map, bnd_count, axis, count, stride)
    for b in range(early.shape[1] // bs):
        early[:, b * bs : (b + 1) * bs] = block_row(lambda col: field[col], blocks, columns, b)


def late_kernel(refs):
    early, field, blocks, table, volume, columns, sems = refs
    (copy,) = to_scalars([table], [columns], sems)
    bs = field.shape[-1]
    first = early.shape[1] // bs
    volume[:, : first * bs] = early[...]
    copy.wait()
    for b in range(first, blocks.shape[0]):
        volume[:, b * bs : (b + 1) * bs] = block_row(lambda col: field[col], blocks, columns, b)


def dense_kernel(vol_size, row_size, col_size, refs):
    near_blocks, table, far_u, far_v, surf_rhs, surf_inverse, dense, *messages, near_cols, sems = refs
    (copy,) = to_scalars([table], [near_cols], sems)
    bs = near_blocks.shape[-1]
    rows = near_blocks.shape[0]
    subs = rows // col_size
    pair = pair_size(row_size)
    chips = row_size // pair
    vol, row, col = (lax.axis_index(name) for name in ("vol", "row", "col"))

    def place(number):
        piece = number // subs
        from_row = lax.rem(piece, row_size)
        chip_slot = slot_of(row // pair, from_row // pair, chips)
        pair_slot = slot_of(lax.rem(row, pair), lax.rem(from_row, pair), pair)
        vol_slot = slot_of(vol, piece // row_size, vol_size)
        slot = (chip_slot * pair + pair_slot) * vol_size + vol_slot
        return slot * subs + lax.rem(number, subs)

    total = vol_size * row_size * subs
    part = total * bs // chips
    together = 2 - rows % 2
    for first in range(0, rows, together):
        numbers = [
            lax.rem(col + at // subs, col_size) * subs + at % subs
            for at in range(first, first + together)
        ]
        u = jnp.concatenate([far_u[0, :, block(b, bs)] for b in numbers], axis=1)
        cols = slice(first * bs, (first + together) * bs)

        def far(number, _):
            v = far_v[0, 0, :, block(number, bs)]
            dense[block(place(number), bs), cols] = lax.dot_general(
                v, u, (((0,), (0,)), ((), ())), preferred_element_type=F32
            ).astype(HALF)
            return _

        lax.fori_loop(0, total, far, 0, unroll=min(total, UNROLL))
        if first == 0:
            copy.wait()
        for i, b in enumerate(numbers):
            cols = slice((first + i) * bs, (first + i + 1) * bs)
            for n in range(near_blocks.shape[2]):
                where = (block(place(near_cols[b, 0, n]), bs), cols)
                near = near_blocks[b, 0, n].astype(F32).T
                dense[where] = (dense[where].astype(F32) + near).astype(HALF)
    width = subs * bs
    for a in range(chips):
        for k in range(col_size):
            if a or k:
                messages[a * col_size + k - 1][0:part, :] = dense[
                    a * part : (a + 1) * part, k * width : (k + 1) * width
                ]
    angles = surf_rhs.shape[0]
    for k in range(1, col_size):
        message = messages[k - 1]
        message[part : part + angles, :] = surf_rhs[...]
        for sub in range(subs):
            at = part + angles + sub * bs
            message[at : at + bs, sub * bs : (sub + 1) * bs] = surf_inverse[sub]


def to_scalars(tables, held, sems):
    copies = [
        pltpu.make_async_copy(table, to, sems.at[i])
        for i, (table, to) in enumerate(zip(tables, held, strict=True))
    ]
    for c in copies:
        c.start()
    return copies


def add_received(total, received):
    for r in received:
        total = total + r[-total.shape[0] :, :].astype(F32)
    return total


def integral_kernel(row_size, vol_size, col_size, refs):
    pair = pair_size(row_size)
    groups = refs[row_size - pair : row_size][::-1] + refs[: row_size - pair]
    refs = refs[row_size:]
    dense, own_trace, *received, _, parts, message = refs
    angles, width = own_trace.shape
    field = jnp.concatenate(
        [g[k * angles : (k + 1) * angles, :] for g in groups for k in range(vol_size)], axis=1
    )
    part = by_cols(field, dense[...])
    for k in range(col_size):
        rows = slice(k * angles, (k + 1) * angles)
        term = part[:, k * width : (k + 1) * width]
        if k == 0:
            term = term + add_received(own_trace[...], received)
        parts[rows, :] = term
        message[rows, :] = term.astype(HALF)


def step_kernel(col_size, refs):
    parts, surf_rhs, surf_inverse, total, *refs = refs
    neighbours, refs = refs[: col_size - 1], refs[col_size - 1 :]
    messages, refs = refs[: col_size - 1], refs[col_size - 1 :]
    surface, half, next_trace, *payloads = refs
    angles = surf_rhs.shape[0]
    bs = surf_inverse.shape[-1]
    subs = surf_inverse.shape[0]
    for j in range(col_size):
        taken = parts[j * angles : (j + 1) * angles, :]
        for shift, message in enumerate(messages, 1):
            k = (j + shift) % col_size
            taken = taken + message[k * angles : (k + 1) * angles, :].astype(F32)
        source = None if j == 0 else neighbours[col_size - j - 1]
        first = 0 if j == 0 else source.shape[0] - angles - subs * bs
        for sub in range(subs):
            cols = slice(sub * bs, (sub + 1) * bs)
            if j == 0:
                rhs, inverse = surf_rhs[:, cols], surf_inverse[sub]
            else:
                at = first + angles + sub * bs
                rhs, inverse = source[first : first + angles, cols], source[at : at + bs, cols]
            resid = (rhs.astype(F32) - taken[:, cols]).astype(HALF)
            value = by_rows(rhs, inverse) + by_rows(resid, inverse)
            if j == 0:
                surface[:, cols] = value
            half[j * angles : (j + 1) * angles, cols] = value.astype(HALF)
    next_trace[...] = total[0]
    send_out(payloads, half[...], total)


def last_integral_kernel(pair, vol_size, col_size, chips, refs):
    groups, refs = refs[:pair], refs[pair:]
    dense, refs = refs[0], refs[1:]
    blocks, outs = refs[: chips * col_size - 1], refs[chips * col_size - 1 :][-chips:]
    angles, width = outs[0].shape
    part = dense.shape[0] // chips
    total = jnp.zeros((angles, chips * width), F32)
    for b in range(col_size):
        place = (col_size - b) % col_size
        field = []
        for g in groups:
            for k in range(vol_size):
                at = (k * col_size + place) * angles
                field.append(g[at : at + angles, :])
        matrix = []
        for a in range(chips):
            own = a == 0 and b == 0
            source = dense if own else blocks[a * col_size + b - 1]
            matrix.append(source[0:part, 0:width])
        total = total + by_cols(
            jnp.concatenate(field, axis=1), jnp.concatenate(matrix, axis=1)
        )
    for a, out in enumerate(outs):
        out[...] = total[:, a * width : (a + 1) * width].astype(out.dtype)


def last_kernel(sums, refs):
    surface, surf_rhs, surf_inverse, integral, own_trace, *refs = refs
    sums, received, out = refs[:sums], refs[sums:-1], refs[-1]
    bs = surf_inverse.shape[-1]
    taken = add_received(integral[...] + own_trace[...], received)
    for s in sums:
        taken = taken + s[...].astype(F32)
    resid = (surf_rhs[...].astype(F32) - taken).astype(HALF)
    for b in range(surf_inverse.shape[0]):
        cols = slice(b * bs, (b + 1) * bs)
        out[:, cols] = surface[:, cols] + by_rows(resid[:, cols], surf_inverse[b])


VMEM = pl.BlockSpec(memory_space=pltpu.VMEM)
SMEM = pl.BlockSpec(memory_space=pltpu.SMEM)


ANY = pl.BlockSpec(memory_space=pl.ANY)
HBM = pl.BlockSpec(memory_space=pltpu.HBM)


def call(body, name, in_specs, outs, flops, moved, scratch=()):
    def kernel(*refs):
        body(refs)

    return pl.pallas_call(
        kernel,
        name=name,
        out_shape=outs,
        in_specs=in_specs,
        out_specs=[VMEM] * len(outs),
        scratch_shapes=list(scratch),
        cost_estimate=pl.CostEstimate(flops=flops, bytes_accessed=moved, transcendentals=0),
        compiler_params=pltpu.CompilerParams(vmem_limit_bytes=48 << 20),
    )


def in_hbm(operand):
    return pltpu.with_memory_space_constraint(operand, pltpu.HBM)


def shifted(value, axis, shift):
    size = lax.axis_size(axis)
    return lax.ppermute(value, axis, [(i, (i + shift) % size) for i in range(size)])


def shifted_in_plane(value, chip, core=0, col=0):
    rows, cols = lax.axis_size("row"), lax.axis_size("col")
    pair = pair_size(rows)
    chips = rows // pair
    pairs = []
    for r in range(rows):
        to = (r // pair + chip) % chips * pair + (r % pair + core) % pair
        pairs += [(r * cols + c, to * cols + (c + col) % cols) for c in range(cols)]
    return lax.ppermute(value, ("row", "col"), pairs)


def local(
    vol_rhs,
    surf_rhs,
    vol_blocks,
    vol_cols,
    coupling,
    trace_map,
    bnd_count,
    surf_inverse,
    near_blocks,
    near_cols,
    far_u,
    far_v,
):
    angles, width = surf_rhs.shape
    vol_count, terms, bs, _ = vol_blocks.shape
    slots = coupling.shape[0]
    nv, nr, nc = (lax.axis_size(a) for a in ("vol", "row", "col"))
    piece = (angles, width)
    product = 2 * angles * bs * bs

    def shape(dims, dtype):
        return jax.ShapeDtypeStruct(dims, dtype)

    tables = (vol_cols.T, trace_map)
    payload_shapes = [shape((2 * angles, width), HALF)] * (nv - 1)
    start_shapes = [shape(piece, HALF), shape(piece, F32)] + payload_shapes
    totals = pltpu.VMEM((nv,) + piece, F32)
    field = pltpu.VMEM((vol_count, angles, bs), HALF)
    scalars = [pltpu.SMEM(t.shape, jnp.int32) for t in tables] + [pltpu.SemaphoreType.DMA((2,))]

    kept = (near_blocks, near_cols, far_u, far_v)
    loaded = (surf_rhs, surf_inverse, vol_rhs, jax.ShapeDtypeStruct((slots, terms, bs, bs), HALF), coupling)
    started = call(
        functools.partial(start_kernel, "vol", len(start_shapes), len(kept)),
        "start",
        [SMEM] + [HBM] * (7 + len(kept)),
        start_shapes + [pltpu.VMEM(a.shape, a.dtype) for a in loaded + tables + kept],
        product * slots * (terms + 1),
        2 * bs * bs * slots * (terms + 1),
        [
            *(pltpu.SMEM(t.shape, jnp.int32) for t in tables),
            totals,
            pltpu.SemaphoreType.DMA((8 + slots + len(kept),)),
        ],
    )(bnd_count, *map(in_hbm, (surf_rhs, surf_inverse, vol_rhs, vol_blocks, coupling) + tables + kept))
    half, own_trace, *payloads = started[: len(start_shapes)]
    surf_rhs, surf_inverse, vol_rhs, boundary_blocks, coupling, *kept = started[len(start_shapes) :]
    tables, kept = (*kept[:2], bnd_count), (*kept[2:], surf_rhs, surf_inverse)

    pair = pair_size(nr)
    chips = nr // pair
    part = nv * pair * width
    sizes = [
        part + (angles + surf_inverse.shape[0] * bs if a == 0 else 0)
        for a in range(chips)
        for b in range(nc)
    ]
    dense, *messages = call(
        functools.partial(dense_kernel, nv, nr, nc),
        "dense",
        [VMEM] * 6,
        [shape((nv * nr * width, nc * width), HALF)]
        + [shape((size, width), HALF) for size in sizes[1:]],
        product * nv * nr * nc,
        4 * nv * nr * nc * bs * bs,
        [
            pltpu.SMEM(near_cols.shape, jnp.int32),
            pltpu.SemaphoreType.DMA((1,)),
        ],
    )(*kept)

    received = [shifted(payloads[k - 1], "vol", k) for k in range(1, nv)]
    blocks = [
        shifted_in_plane(messages[i - 1], chip=-(i // nc), col=i % nc) for i in range(1, nc)
    ]
    group = jnp.concatenate([half] + [r[:angles] for r in received], axis=0)
    group, dense = lax.optimization_barrier((group, dense))
    groups = [group] + [
        shifted_in_plane(group, chip=i // pair, core=i % pair) for i in range(1, nr)
    ]
    (total,) = call(
        functools.partial(boundary_kernel, "vol"),
        "boundary",
        [VMEM] * 6 + [SMEM],
        [shape((nv,) + piece, F32)],
        product * slots * (terms + 2),
        2 * bs * bs * slots * (terms + 1),
        [field] + scalars,
    )(group, vol_rhs, boundary_blocks, coupling, *tables)
    ahead = [
        shifted_in_plane(messages[i - 1], chip=-(i // nc), col=0) for i in range(nc, nc * chips, nc)
    ]
    parts, message = call(
        functools.partial(integral_kernel, nr, nv, nc),
        "integral",
        [VMEM] * (nr + nv + 1) + [ANY],
        [shape((nc * angles, width), F32), shape((nc * angles, width), HALF)],
        INTEGRAL_COST,
        2 * nv * nr * nc * width * width,
    )(*groups[pair:], *groups[:pair][::-1], dense, own_trace, *received, total)
    sums = [shifted(message, "col", k) for k in range(1, nc)]
    parts, vol_blocks, *later = lax.optimization_barrier(
        (parts, vol_blocks, *(messages[i - 1] for i in range(nc, nc * chips) if i % nc))
    )
    later = iter(later)
    after = {
        i: shifted_in_plane(next(later), chip=-(i // nc), col=i % nc)
        for i in range(nc, nc * chips)
        if i % nc
    }
    surface, half, own_trace, *payloads = call(
        functools.partial(step_kernel, nc),
        "step",
        [VMEM] * (4 + 2 * (nc - 1)),
        [shape(piece, F32), shape((nc * angles, width), HALF), shape(piece, F32)]
        + [shape(((nc + 1) * angles, width), HALF)] * (nv - 1),
        STEP_COST,
        nc << 17,
    )(parts, surf_rhs, surf_inverse, total, *blocks, *sums)

    received = [shifted(payloads[k - 1], "vol", k) for k in range(1, nv)]
    received, ahead = lax.optimization_barrier((received[1:] + received[:1], ahead))
    received = received[-1:] + received[:-1]
    group = jnp.concatenate([half] + [r[: nc * angles] for r in received], axis=0)
    group, after = lax.optimization_barrier((group, after))
    blocks += [
        after[i] if i % nc else ahead[i // nc - 1] for i in range(nc, nc * chips)
    ]
    groups = [group] + [shifted_in_plane(group, chip=0, core=k) for k in range(1, pair)]
    split = vol_count // 3
    early, residual = call(
        functools.partial(early_kernel, "vol", nv, nc),
        "early_volume",
        [VMEM] * 6 + [SMEM],
        [shape((angles, split * bs), F32), shape((vol_count, angles, bs), HALF)],
        product * split * terms,
        2 * bs * bs * split * terms,
        scalars,
    )(group, vol_rhs, vol_blocks, coupling, *tables)
    integral, *parts = call(
        functools.partial(last_integral_kernel, pair, nv, nc, chips),
        "last_integral",
        [VMEM] * (pair + chips * nc) + [ANY],
        [shape(piece, F32)] + [shape(piece, HALF)] * (chips - 1),
        product * nv * nr * nc,
        2 * nv * nr * nc * width * width,
    )(*groups, dense, *blocks, early)
    sums = [shifted_in_plane(parts[a - 1], chip=a) for a in range(1, chips)]
    (volume,) = call(
        late_kernel,
        "late_volume",
        [VMEM] * 4,
        [shape((angles, vol_count * bs), F32)],
        product * (vol_count - split) * terms,
        2 * bs * bs * (vol_count - split) * terms,
        [scalars[0], pltpu.SemaphoreType.DMA((1,))],
    )(early, residual, vol_blocks, tables[0])
    (surface,) = call(
        functools.partial(last_kernel, chips - 1),
        "last",
        [VMEM] * (5 + chips - 1 + nv - 1),
        [shape(piece, F32)],
        product,
        1 << 17,
    )(surface, surf_rhs, surf_inverse, integral, own_trace, *sums, *received)
    return volume, surface


def solution(mesh):
    everywhere = ("vol", "row", "col")
    in_specs = (
        P(None, everywhere),
        P(None, everywhere),
        P(everywhere, None, None, None),
        P(everywhere, None),
        P(everywhere, None, None),
        P(everywhere),
        P(everywhere),
        P(everywhere, None, None),
        P(("vol", "row"), "col", None, None, None),
        P(("vol", "row"), "col", None),
        P("col", None, ("vol", "row")),
        P(("vol", "row"), "col", None, None),
    )
    out_specs = (P(None, everywhere), P(None, everywhere))
    return jax.shard_map(local, mesh=mesh, in_specs=in_specs, out_specs=out_specs, check_vma=False)
```

```python
import functools

import jax
import jax.numpy as jnp
from jax import lax
from jax.experimental import pallas as pl
from jax.experimental.pallas import tpu as pltpu
from jax.sharding import PartitionSpec as P

UNROLL = 16
INTEGRAL_COST = 10**9
STEP_COST = 10**9
F32 = jnp.float32
HALF = jnp.bfloat16


def by_rows(a, b):
    return lax.dot_general(a, b, (((1,), (1,)), ((), ())), preferred_element_type=F32)


def by_cols(a, b):
    return lax.dot_general(a, b, (((1,), (0,)), ((), ())), preferred_element_type=F32)


def block(start, size):
    return pl.ds(pl.multiple_of(start * size, size), size)


def slot_of(index, here, count):
    return lax.rem(index - here + count, count)


def pair_size(rows):
    return 2 if rows % 2 == 0 else 1


def block_row(read, blocks, columns, row):
    terms = blocks.shape[1]
    field = jnp.concatenate([read(columns[n, row]) for n in range(terms)], axis=1)
    inverse = jnp.concatenate([blocks[row, n] for n in range(terms)], axis=1)
    return by_rows(field, inverse)


def add_traces(total, boundary, coupling, trace_map, bnd_count, axis):
    count = total.shape[0]
    bs = coupling.shape[-1]
    subs = total.shape[2] // bs
    here = lax.axis_index(axis)
    for j in range(coupling.shape[0]):
        alive = (j < bnd_count[0]).astype(F32)
        contrib = by_cols(boundary(j), coupling[j]) * alive
        target = trace_map[j]
        slot = slot_of(target // subs, here, count)
        where = (slot, slice(None), block(lax.rem(target, subs), bs))
        total[where] = total[where] + contrib


def residual_blocks(resid, vol_rhs, group, coupling, trace_map, bnd_count, axis, count, stride):
    bs = coupling.shape[-1]
    angles = vol_rhs.shape[0]
    subs = group.shape[1] // bs
    here = lax.axis_index(axis)
    for j in range(coupling.shape[0]):
        alive = (j < bnd_count[0]).astype(F32)
        target = trace_map[j]
        slot = slot_of(here, target // subs, count)
        picked = group[block(slot * stride, angles), block(lax.rem(target, subs), bs)]
        current = by_rows(picked, coupling[j]) * alive
        rhs = vol_rhs[:, j * bs : (j + 1) * bs].astype(F32)
        resid[j] = (rhs - current).astype(HALF)


def send_out(payloads, half, total):
    rows = half.shape[0]
    for k, payload in enumerate(payloads):
        payload[0:rows, :] = half
        payload[rows:, :] = total[k + 1].astype(HALF)


def start_kernel(axis, outs, kept, refs):
    bnd_count, operands, refs = refs[0], refs[1 : 8 + kept], refs[8 + kept :]
    half_out, own_trace, *payloads = refs[:outs]
    loaded, copied, refs = refs[outs : outs + 5], refs[outs + 5 : outs + 7 + kept], refs[outs + 7 + kept :]
    surf_rhs, surf_inverse, vol_rhs, blocks, coupling = loaded
    columns, trace_map, total, sems = refs
    slots = coupling.shape[0]
    bs = coupling.shape[-1]
    count = iter(range(sems.shape[0]))

    def copy(source, to):
        started = pltpu.make_async_copy(source, to, sems.at[next(count)])
        started.start()
        return started

    tables = [copy(operands[5 + i], t) for i, t in enumerate((columns, trace_map))]
    first = [copy(operands[0], surf_rhs), copy(operands[1], surf_inverse)]
    tables.append(copy(operands[2], vol_rhs))
    rows = [copy(operands[3].at[j], blocks.at[j]) for j in range(slots)]
    last = copy(operands[4], coupling)
    later = [copy(operands[5 + i], t) for i, t in enumerate(copied)]
    total[...] = jnp.zeros_like(total)
    for c in first:
        c.wait()
    for b in range(surf_inverse.shape[0]):
        cols = slice(b * bs, (b + 1) * bs)
        half_out[:, cols] = by_rows(surf_rhs[:, cols], surf_inverse[b]).astype(HALF)
    for c in tables:
        c.wait()
    solved = []
    for j in range(slots):
        rows[j].wait()
        read = lambda col: vol_rhs[:, block(col, bs)]
        solved.append(block_row(read, blocks, columns, j).astype(HALF))
    last.wait()
    add_traces(total, lambda j: solved[j], coupling, trace_map, bnd_count, axis)
    own_trace[...] = total[0]
    send_out(payloads, half_out[...], total)
    for c in later:
        c.wait()


def boundary_kernel(axis, refs):
    group, vol_rhs, blocks, coupling, *tables, bnd_count, total, field, columns, trace_map, sems = refs
    copies = to_scalars(tables, (columns, trace_map), sems)
    bs = coupling.shape[-1]
    slots = coupling.shape[0]
    count = total.shape[0]
    for b in range(slots, vol_rhs.shape[1] // bs):
        field[b] = vol_rhs[:, b * bs : (b + 1) * bs]
    total[...] = jnp.zeros_like(total)
    for c in copies:
        c.wait()
    residual_blocks(field, vol_rhs, group, coupling, trace_map, bnd_count, axis, count, 1)

    def boundary(j):
        return block_row(lambda col: field[col], blocks, columns, j).astype(HALF)

    add_traces(total, boundary, coupling, trace_map, bnd_count, axis)


def base_kernel(refs):
    vol_rhs, blocks, table, base, matrix, columns, sems = refs
    (copy,) = to_scalars([table], [columns], sems)
    bs = blocks.shape[-1]
    slots = matrix.shape[1] // bs - 1
    matrix[...] = jnp.zeros_like(matrix)
    copy.wait()
    for b in range(blocks.shape[0]):
        rows = slice(b * bs, (b + 1) * bs)
        for n in range(blocks.shape[1]):
            matrix[rows, block(lax.min(columns[n, b], slots), bs)] = blocks[b, n]
        read = lambda col: vol_rhs[:, block(col, bs)]
        base[:, rows] = block_row(read, blocks, columns, b)


def volume_kernel(axis, count, stride, refs):
    group, coupling, table, bnd_count, base, matrix, volume, trace_map, sems = refs
    copies = to_scalars([table], [trace_map], sems)
    slots, bs, _ = coupling.shape
    angles = volume.shape[0]
    subs = group.shape[1] // bs
    here = lax.axis_index(axis)
    for c in copies:
        c.wait()
    currents = []
    for j in range(slots):
        alive = (j < bnd_count[0]).astype(F32)
        target = trace_map[j]
        slot = slot_of(here, target // subs, count)
        picked = group[block(slot * stride, angles), block(lax.rem(target, subs), bs)]
        currents.append((by_rows(picked, coupling[j]) * alive).astype(HALF))
    current = jnp.concatenate(currents, axis=1)
    for first in range(0, volume.shape[1], 2 * bs):
        part = slice(first, min(first + 2 * bs, volume.shape[1]))
        volume[:, part] = base[:, part] - by_rows(current, matrix[part, 0 : slots * bs])


def dense_kernel(vol_size, row_size, col_size, refs):
    near_blocks, table, far_u, far_v, surf_rhs, surf_inverse, dense, *messages, near_cols, sems = refs
    (copy,) = to_scalars([table], [near_cols], sems)
    bs = near_blocks.shape[-1]
    rows = near_blocks.shape[0]
    subs = rows // col_size
    pair = pair_size(row_size)
    chips = row_size // pair
    vol, row, col = (lax.axis_index(name) for name in ("vol", "row", "col"))

    def place(number):
        piece = number // subs
        from_row = lax.rem(piece, row_size)
        chip_slot = slot_of(row // pair, from_row // pair, chips)
        pair_slot = slot_of(lax.rem(row, pair), lax.rem(from_row, pair), pair)
        vol_slot = slot_of(vol, piece // row_size, vol_size)
        slot = (chip_slot * pair + pair_slot) * vol_size + vol_slot
        return slot * subs + lax.rem(number, subs)

    total = vol_size * row_size * subs
    part = total * bs // chips
    together = 2 - rows % 2
    for first in range(0, rows, together):
        numbers = [
            lax.rem(col + at // subs, col_size) * subs + at % subs
            for at in range(first, first + together)
        ]
        u = jnp.concatenate([far_u[0, :, block(b, bs)] for b in numbers], axis=1)
        cols = slice(first * bs, (first + together) * bs)

        def far(number, _):
            v = far_v[0, 0, :, block(number, bs)]
            dense[block(place(number), bs), cols] = lax.dot_general(
                v, u, (((0,), (0,)), ((), ())), preferred_element_type=F32
            ).astype(HALF)
            return _

        lax.fori_loop(0, total, far, 0, unroll=min(total, UNROLL))
        if first == 0:
            copy.wait()
        for i, b in enumerate(numbers):
            cols = slice((first + i) * bs, (first + i + 1) * bs)
            for n in range(near_blocks.shape[2]):
                where = (block(place(near_cols[b, 0, n]), bs), cols)
                near = near_blocks[b, 0, n].astype(F32).T
                dense[where] = (dense[where].astype(F32) + near).astype(HALF)
    width = subs * bs
    for a in range(chips):
        for k in range(col_size):
            if a or k:
                messages[a * col_size + k - 1][0:part, :] = dense[
                    a * part : (a + 1) * part, k * width : (k + 1) * width
                ]
    angles = surf_rhs.shape[0]
    for k in range(1, col_size):
        message = messages[k - 1]
        message[part : part + angles, :] = surf_rhs[...]
        for sub in range(subs):
            at = part + angles + sub * bs
            message[at : at + bs, sub * bs : (sub + 1) * bs] = surf_inverse[sub]


def to_scalars(tables, held, sems):
    copies = [
        pltpu.make_async_copy(table, to, sems.at[i])
        for i, (table, to) in enumerate(zip(tables, held, strict=True))
    ]
    for c in copies:
        c.start()
    return copies


def add_received(total, received):
    for r in received:
        total = total + r[-total.shape[0] :, :].astype(F32)
    return total


def integral_kernel(row_size, vol_size, col_size, refs):
    pair = pair_size(row_size)
    groups = refs[row_size - pair : row_size][::-1] + refs[: row_size - pair]
    refs = refs[row_size:]
    dense, own_trace, *received, _, parts, message = refs
    angles, width = own_trace.shape
    field = jnp.concatenate(
        [g[k * angles : (k + 1) * angles, :] for g in groups for k in range(vol_size)], axis=1
    )
    part = by_cols(field, dense[...])
    for k in range(col_size):
        rows = slice(k * angles, (k + 1) * angles)
        term = part[:, k * width : (k + 1) * width]
        if k == 0:
            term = term + add_received(own_trace[...], received)
        parts[rows, :] = term
        message[rows, :] = term.astype(HALF)


def step_kernel(col_size, refs):
    parts, surf_rhs, surf_inverse, total, *refs = refs
    neighbours, refs = refs[: col_size - 1], refs[col_size - 1 :]
    messages, refs = refs[: col_size - 1], refs[col_size - 1 :]
    surface, half, next_trace, *payloads = refs
    angles = surf_rhs.shape[0]
    bs = surf_inverse.shape[-1]
    subs = surf_inverse.shape[0]
    for j in range(col_size):
        taken = parts[j * angles : (j + 1) * angles, :]
        for shift, message in enumerate(messages, 1):
            k = (j + shift) % col_size
            taken = taken + message[k * angles : (k + 1) * angles, :].astype(F32)
        source = None if j == 0 else neighbours[col_size - j - 1]
        first = 0 if j == 0 else source.shape[0] - angles - subs * bs
        for sub in range(subs):
            cols = slice(sub * bs, (sub + 1) * bs)
            if j == 0:
                rhs, inverse = surf_rhs[:, cols], surf_inverse[sub]
            else:
                at = first + angles + sub * bs
                rhs, inverse = source[first : first + angles, cols], source[at : at + bs, cols]
            resid = (rhs.astype(F32) - taken[:, cols]).astype(HALF)
            value = by_rows(rhs, inverse) + by_rows(resid, inverse)
            if j == 0:
                surface[:, cols] = value
            half[j * angles : (j + 1) * angles, cols] = value.astype(HALF)
    next_trace[...] = total[0]
    send_out(payloads, half[...], total)


def last_integral_kernel(pair, vol_size, col_size, chips, refs):
    groups, refs = refs[:pair], refs[pair:]
    dense, refs = refs[0], refs[1:]
    blocks, outs = refs[: chips * col_size - 1], refs[chips * col_size - 1 :][-chips:]
    angles, width = outs[0].shape
    part = dense.shape[0] // chips
    total = jnp.zeros((angles, chips * width), F32)
    for b in range(col_size):
        place = (col_size - b) % col_size
        field = []
        for g in groups:
            for k in range(vol_size):
                at = (k * col_size + place) * angles
                field.append(g[at : at + angles, :])
        matrix = []
        for a in range(chips):
            own = a == 0 and b == 0
            source = dense if own else blocks[a * col_size + b - 1]
            matrix.append(source[0:part, 0:width])
        total = total + by_cols(
            jnp.concatenate(field, axis=1), jnp.concatenate(matrix, axis=1)
        )
    for a, out in enumerate(outs):
        out[...] = total[:, a * width : (a + 1) * width].astype(out.dtype)


def last_kernel(sums, refs):
    surface, surf_rhs, surf_inverse, integral, own_trace, *refs = refs
    sums, received, out = refs[:sums], refs[sums:-1], refs[-1]
    bs = surf_inverse.shape[-1]
    taken = add_received(integral[...] + own_trace[...], received)
    for s in sums:
        taken = taken + s[...].astype(F32)
    resid = (surf_rhs[...].astype(F32) - taken).astype(HALF)
    for b in range(surf_inverse.shape[0]):
        cols = slice(b * bs, (b + 1) * bs)
        out[:, cols] = surface[:, cols] + by_rows(resid[:, cols], surf_inverse[b])


VMEM = pl.BlockSpec(memory_space=pltpu.VMEM)
SMEM = pl.BlockSpec(memory_space=pltpu.SMEM)


ANY = pl.BlockSpec(memory_space=pl.ANY)
HBM = pl.BlockSpec(memory_space=pltpu.HBM)


def call(body, name, in_specs, outs, flops, moved, scratch=()):
    def kernel(*refs):
        body(refs)

    return pl.pallas_call(
        kernel,
        name=name,
        out_shape=outs,
        in_specs=in_specs,
        out_specs=[VMEM] * len(outs),
        scratch_shapes=list(scratch),
        cost_estimate=pl.CostEstimate(flops=flops, bytes_accessed=moved, transcendentals=0),
        compiler_params=pltpu.CompilerParams(vmem_limit_bytes=48 << 20),
    )


def in_hbm(operand):
    return pltpu.with_memory_space_constraint(operand, pltpu.HBM)


def shifted(value, axis, shift):
    size = lax.axis_size(axis)
    return lax.ppermute(value, axis, [(i, (i + shift) % size) for i in range(size)])


def shifted_in_plane(value, chip, core=0, col=0):
    rows, cols = lax.axis_size("row"), lax.axis_size("col")
    pair = pair_size(rows)
    chips = rows // pair
    pairs = []
    for r in range(rows):
        to = (r // pair + chip) % chips * pair + (r % pair + core) % pair
        pairs += [(r * cols + c, to * cols + (c + col) % cols) for c in range(cols)]
    return lax.ppermute(value, ("row", "col"), pairs)


def local(
    vol_rhs,
    surf_rhs,
    vol_blocks,
    vol_cols,
    coupling,
    trace_map,
    bnd_count,
    surf_inverse,
    near_blocks,
    near_cols,
    far_u,
    far_v,
):
    angles, width = surf_rhs.shape
    vol_count, terms, bs, _ = vol_blocks.shape
    slots = coupling.shape[0]
    nv, nr, nc = (lax.axis_size(a) for a in ("vol", "row", "col"))
    piece = (angles, width)
    product = 2 * angles * bs * bs

    def shape(dims, dtype):
        return jax.ShapeDtypeStruct(dims, dtype)

    tables = (vol_cols.T, trace_map)
    payload_shapes = [shape((2 * angles, width), HALF)] * (nv - 1)
    start_shapes = [shape(piece, HALF), shape(piece, F32)] + payload_shapes
    totals = pltpu.VMEM((nv,) + piece, F32)
    field = pltpu.VMEM((vol_count, angles, bs), HALF)
    scalars = [pltpu.SMEM(t.shape, jnp.int32) for t in tables] + [pltpu.SemaphoreType.DMA((2,))]

    kept = (near_blocks, near_cols, far_u, far_v)
    loaded = (surf_rhs, surf_inverse, vol_rhs, jax.ShapeDtypeStruct((slots, terms, bs, bs), HALF), coupling)
    started = call(
        functools.partial(start_kernel, "vol", len(start_shapes), len(kept)),
        "start",
        [SMEM] + [HBM] * (7 + len(kept)),
        start_shapes + [pltpu.VMEM(a.shape, a.dtype) for a in loaded + tables + kept],
        product * slots * (terms + 1),
        2 * bs * bs * slots * (terms + 1),
        [
            *(pltpu.SMEM(t.shape, jnp.int32) for t in tables),
            totals,
            pltpu.SemaphoreType.DMA((8 + slots + len(kept),)),
        ],
    )(bnd_count, *map(in_hbm, (surf_rhs, surf_inverse, vol_rhs, vol_blocks, coupling) + tables + kept))
    half, own_trace, *payloads = started[: len(start_shapes)]
    surf_rhs, surf_inverse, vol_rhs, boundary_blocks, coupling, *kept = started[len(start_shapes) :]
    tables, kept = (*kept[:2], bnd_count), (*kept[2:], surf_rhs, surf_inverse)

    pair = pair_size(nr)
    chips = nr // pair
    part = nv * pair * width
    sizes = [
        part + (angles + surf_inverse.shape[0] * bs if a == 0 else 0)
        for a in range(chips)
        for b in range(nc)
    ]
    dense, *messages = call(
        functools.partial(dense_kernel, nv, nr, nc),
        "dense",
        [VMEM] * 6,
        [shape((nv * nr * width, nc * width), HALF)]
        + [shape((size, width), HALF) for size in sizes[1:]],
        product * nv * nr * nc,
        4 * nv * nr * nc * bs * bs,
        [
            pltpu.SMEM(near_cols.shape, jnp.int32),
            pltpu.SemaphoreType.DMA((1,)),
        ],
    )(*kept)

    received = [shifted(payloads[k - 1], "vol", k) for k in range(1, nv)]
    blocks = [
        shifted_in_plane(messages[i - 1], chip=-(i // nc), col=i % nc) for i in range(1, nc)
    ]
    group = jnp.concatenate([half] + [r[:angles] for r in received], axis=0)
    group, dense = lax.optimization_barrier((group, dense))
    groups = [group] + [
        shifted_in_plane(group, chip=i // pair, core=i % pair) for i in range(1, nr)
    ]
    (total,) = call(
        functools.partial(boundary_kernel, "vol"),
        "boundary",
        [VMEM] * 6 + [SMEM],
        [shape((nv,) + piece, F32)],
        product * slots * (terms + 2),
        2 * bs * bs * slots * (terms + 1),
        [field] + scalars,
    )(group, vol_rhs, boundary_blocks, coupling, *tables)
    ahead = [
        shifted_in_plane(messages[i - 1], chip=-(i // nc), col=0) for i in range(nc, nc * chips, nc)
    ]
    parts, message = call(
        functools.partial(integral_kernel, nr, nv, nc),
        "integral",
        [VMEM] * (nr + nv + 1) + [ANY],
        [shape((nc * angles, width), F32), shape((nc * angles, width), HALF)],
        INTEGRAL_COST,
        2 * nv * nr * nc * width * width,
    )(*groups[pair:], *groups[:pair][::-1], dense, own_trace, *received, total)
    sums = [shifted(message, "col", k) for k in range(1, nc)]
    parts, vol_blocks, *later = lax.optimization_barrier(
        (parts, vol_blocks, *(messages[i - 1] for i in range(nc, nc * chips) if i % nc))
    )
    later = iter(later)
    after = {
        i: shifted_in_plane(next(later), chip=-(i // nc), col=i % nc)
        for i in range(nc, nc * chips)
        if i % nc
    }
    surface, half, own_trace, *payloads = call(
        functools.partial(step_kernel, nc),
        "step",
        [VMEM] * (4 + 2 * (nc - 1)),
        [shape(piece, F32), shape((nc * angles, width), HALF), shape(piece, F32)]
        + [shape(((nc + 1) * angles, width), HALF)] * (nv - 1),
        STEP_COST,
        nc << 17,
    )(parts, surf_rhs, surf_inverse, total, *blocks, *sums)

    received = [shifted(payloads[k - 1], "vol", k) for k in range(1, nv)]
    received, ahead = lax.optimization_barrier((received[1:] + received[:1], ahead))
    received = received[-1:] + received[:-1]
    half, vol_blocks = lax.optimization_barrier((half, vol_blocks))
    base, matrix = call(
        base_kernel,
        "base_volume",
        [VMEM] * 3,
        [
            shape((angles, vol_count * bs), F32),
            shape((vol_count * bs, (slots + 1) * bs), HALF),
        ],
        product * vol_count * terms,
        2 * bs * bs * vol_count * terms,
        [scalars[0], pltpu.SemaphoreType.DMA((1,))],
    )(vol_rhs, vol_blocks, tables[0])
    group = jnp.concatenate([half] + [r[: nc * angles] for r in received], axis=0)
    group, after = lax.optimization_barrier((group, after))
    blocks += [
        after[i] if i % nc else ahead[i // nc - 1] for i in range(nc, nc * chips)
    ]
    group, base = lax.optimization_barrier((group, base))
    groups = [group] + [shifted_in_plane(group, chip=0, core=k) for k in range(1, pair)]
    integral, *parts = call(
        functools.partial(last_integral_kernel, pair, nv, nc, chips),
        "last_integral",
        [VMEM] * (pair + chips * nc),
        [shape(piece, F32)] + [shape(piece, HALF)] * (chips - 1),
        product * nv * nr * nc,
        2 * nv * nr * nc * width * width,
    )(*groups, dense, *blocks)
    sums = [shifted_in_plane(parts[a - 1], chip=a) for a in range(1, chips)]
    (volume,) = call(
        functools.partial(volume_kernel, "vol", nv, nc),
        "volume",
        [VMEM] * 3 + [SMEM] + [VMEM] * 2,
        [shape((angles, vol_count * bs), F32)],
        product * slots * (vol_count + 1),
        2 * bs * bs * slots * (vol_count + 1),
        [scalars[1], pltpu.SemaphoreType.DMA((1,))],
    )(group, coupling, tables[1], tables[2], base, matrix)
    (surface,) = call(
        functools.partial(last_kernel, chips - 1),
        "last",
        [VMEM] * (5 + chips - 1 + nv - 1),
        [shape(piece, F32)],
        product,
        1 << 17,
    )(surface, surf_rhs, surf_inverse, integral, own_trace, *sums, *received)
    return volume, surface


def solution(mesh):
    everywhere = ("vol", "row", "col")
    in_specs = (
        P(None, everywhere),
        P(None, everywhere),
        P(everywhere, None, None, None),
        P(everywhere, None),
        P(everywhere, None, None),
        P(everywhere),
        P(everywhere),
        P(everywhere, None, None),
        P(("vol", "row"), "col", None, None, None),
        P(("vol", "row"), "col", None),
        P("col", None, ("vol", "row")),
        P(("vol", "row"), "col", None, None),
    )
    out_specs = (P(None, everywhere), P(None, everywhere))
    return jax.shard_map(local, mesh=mesh, in_specs=in_specs, out_specs=out_specs, check_vma=False)
```

```python
import functools

import jax
import jax.numpy as jnp
from jax import lax
from jax.experimental import pallas as pl
from jax.experimental.pallas import tpu as pltpu
from jax.sharding import PartitionSpec as P

UNROLL = 16
INTEGRAL_COST = 10**9
STEP_COST = 10**9
F32 = jnp.float32
HALF = jnp.bfloat16


def by_rows(a, b):
    return lax.dot_general(a, b, (((1,), (1,)), ((), ())), preferred_element_type=F32)


def by_cols(a, b):
    return lax.dot_general(a, b, (((1,), (0,)), ((), ())), preferred_element_type=F32)


def block(start, size):
    return pl.ds(pl.multiple_of(start * size, size), size)


def slot_of(index, here, count):
    return lax.rem(index - here + count, count)


def pair_size(rows):
    return 2 if rows % 2 == 0 else 1


def block_row(read, blocks, columns, row):
    terms = blocks.shape[1]
    field = jnp.concatenate([read(columns[n, row]) for n in range(terms)], axis=1)
    inverse = jnp.concatenate([blocks[row, n] for n in range(terms)], axis=1)
    return by_rows(field, inverse)


def add_traces(total, boundary, coupling, trace_map, bnd_count, axis):
    count = total.shape[0]
    bs = coupling.shape[-1]
    subs = total.shape[2] // bs
    here = lax.axis_index(axis)
    for j in range(coupling.shape[0]):
        alive = (j < bnd_count[0]).astype(F32)
        contrib = by_cols(boundary(j), coupling[j]) * alive
        target = trace_map[j]
        slot = slot_of(target // subs, here, count)
        where = (slot, slice(None), block(lax.rem(target, subs), bs))
        total[where] = total[where] + contrib


def residual_blocks(resid, vol_rhs, group, coupling, trace_map, bnd_count, axis, count, stride):
    bs = coupling.shape[-1]
    angles = vol_rhs.shape[0]
    subs = group.shape[1] // bs
    here = lax.axis_index(axis)
    for j in range(coupling.shape[0]):
        alive = (j < bnd_count[0]).astype(F32)
        target = trace_map[j]
        slot = slot_of(here, target // subs, count)
        picked = group[block(slot * stride, angles), block(lax.rem(target, subs), bs)]
        current = by_rows(picked, coupling[j]) * alive
        rhs = vol_rhs[:, j * bs : (j + 1) * bs].astype(F32)
        resid[j] = (rhs - current).astype(HALF)


def send_out(payloads, half, total):
    rows = half.shape[0]
    for k, payload in enumerate(payloads):
        payload[0:rows, :] = half
        payload[rows:, :] = total[k + 1].astype(HALF)


def start_kernel(axis, outs, kept, refs):
    bnd_count, operands, refs = refs[0], refs[1 : 8 + kept], refs[8 + kept :]
    half_out, own_trace, *payloads = refs[:outs]
    loaded, copied, refs = refs[outs : outs + 5], refs[outs + 5 : outs + 7 + kept], refs[outs + 7 + kept :]
    surf_rhs, surf_inverse, vol_rhs, blocks, coupling = loaded
    columns, trace_map, total, sems = refs
    slots = coupling.shape[0]
    bs = coupling.shape[-1]
    count = iter(range(sems.shape[0]))

    def copy(source, to):
        started = pltpu.make_async_copy(source, to, sems.at[next(count)])
        started.start()
        return started

    tables = [copy(operands[5 + i], t) for i, t in enumerate((columns, trace_map))]
    first = [copy(operands[0], surf_rhs), copy(operands[1], surf_inverse)]
    tables.append(copy(operands[2], vol_rhs))
    rows = [copy(operands[3].at[j], blocks.at[j]) for j in range(slots)]
    last = copy(operands[4], coupling)
    later = [copy(operands[5 + i], t) for i, t in enumerate(copied)]
    total[...] = jnp.zeros_like(total)
    for c in first:
        c.wait()
    for b in range(surf_inverse.shape[0]):
        cols = slice(b * bs, (b + 1) * bs)
        half_out[:, cols] = by_rows(surf_rhs[:, cols], surf_inverse[b]).astype(HALF)
    for c in tables:
        c.wait()
    solved = []
    for j in range(slots):
        rows[j].wait()
        read = lambda col: vol_rhs[:, block(col, bs)]
        solved.append(block_row(read, blocks, columns, j).astype(HALF))
    last.wait()
    add_traces(total, lambda j: solved[j], coupling, trace_map, bnd_count, axis)
    own_trace[...] = total[0]
    send_out(payloads, half_out[...], total)
    for c in later:
        c.wait()


def boundary_kernel(axis, refs):
    group, vol_rhs, blocks, coupling, *tables, bnd_count, total, field, columns, trace_map, sems = refs
    copies = to_scalars(tables, (columns, trace_map), sems)
    bs = coupling.shape[-1]
    slots = coupling.shape[0]
    count = total.shape[0]
    for b in range(slots, vol_rhs.shape[1] // bs):
        field[b] = vol_rhs[:, b * bs : (b + 1) * bs]
    total[...] = jnp.zeros_like(total)
    for c in copies:
        c.wait()
    residual_blocks(field, vol_rhs, group, coupling, trace_map, bnd_count, axis, count, 1)

    def boundary(j):
        return block_row(lambda col: field[col], blocks, columns, j).astype(HALF)

    add_traces(total, boundary, coupling, trace_map, bnd_count, axis)


def base_kernel(refs):
    vol_rhs, blocks, table, base, matrix, columns, sems = refs
    (copy,) = to_scalars([table], [columns], sems)
    bs = blocks.shape[-1]
    slots = matrix.shape[1] // bs - 1
    matrix[...] = jnp.zeros_like(matrix)
    copy.wait()
    for b in range(blocks.shape[0]):
        rows = slice(b * bs, (b + 1) * bs)
        for n in range(blocks.shape[1]):
            matrix[rows, block(lax.min(columns[n, b], slots), bs)] = blocks[b, n]
        read = lambda col: vol_rhs[:, block(col, bs)]
        base[:, rows] = block_row(read, blocks, columns, b)


def volume_kernel(axis, count, stride, refs):
    group, coupling, table, bnd_count, base, matrix, volume, trace_map, sems = refs
    copies = to_scalars([table], [trace_map], sems)
    slots, bs, _ = coupling.shape
    angles = volume.shape[0]
    subs = group.shape[1] // bs
    here = lax.axis_index(axis)
    for c in copies:
        c.wait()
    currents = []
    for j in range(slots):
        alive = (j < bnd_count[0]).astype(F32)
        target = trace_map[j]
        slot = slot_of(here, target // subs, count)
        picked = group[block(slot * stride, angles), block(lax.rem(target, subs), bs)]
        currents.append((by_rows(picked, coupling[j]) * alive).astype(HALF))
    current = jnp.concatenate(currents, axis=1)
    for first in range(0, volume.shape[1], 2 * bs):
        part = slice(first, min(first + 2 * bs, volume.shape[1]))
        volume[:, part] = base[:, part] - by_rows(current, matrix[part, 0 : slots * bs])


def dense_kernel(vol_size, row_size, col_size, refs):
    near_blocks, table, far_u, far_v, surf_rhs, surf_inverse, dense, *messages, near_cols, sems = refs
    (copy,) = to_scalars([table], [near_cols], sems)
    bs = near_blocks.shape[-1]
    rows = near_blocks.shape[0]
    subs = rows // col_size
    pair = pair_size(row_size)
    chips = row_size // pair
    vol, row, col = (lax.axis_index(name) for name in ("vol", "row", "col"))

    def place(number):
        piece = number // subs
        from_row = lax.rem(piece, row_size)
        chip_slot = slot_of(row // pair, from_row // pair, chips)
        pair_slot = slot_of(lax.rem(row, pair), lax.rem(from_row, pair), pair)
        vol_slot = slot_of(vol, piece // row_size, vol_size)
        slot = (chip_slot * pair + pair_slot) * vol_size + vol_slot
        return slot * subs + lax.rem(number, subs)

    total = vol_size * row_size * subs
    part = total * bs // chips
    together = 2 - rows % 2
    for first in range(0, rows, together):
        numbers = [
            lax.rem(col + at // subs, col_size) * subs + at % subs
            for at in range(first, first + together)
        ]
        u = jnp.concatenate([far_u[0, :, block(b, bs)] for b in numbers], axis=1)
        cols = slice(first * bs, (first + together) * bs)

        def far(number, _):
            v = far_v[0, 0, :, block(number, bs)]
            dense[block(place(number), bs), cols] = lax.dot_general(
                v, u, (((0,), (0,)), ((), ())), preferred_element_type=F32
            ).astype(HALF)
            return _

        lax.fori_loop(0, total, far, 0, unroll=min(total, UNROLL))
        if first == 0:
            copy.wait()
        for i, b in enumerate(numbers):
            cols = slice((first + i) * bs, (first + i + 1) * bs)
            for n in range(near_blocks.shape[2]):
                where = (block(place(near_cols[b, 0, n]), bs), cols)
                near = near_blocks[b, 0, n].astype(F32).T
                dense[where] = (dense[where].astype(F32) + near).astype(HALF)
    width = subs * bs
    for k in range(1, col_size):
        messages[k - 1][0:part, :] = dense[0:part, k * width : (k + 1) * width]
    angles = surf_rhs.shape[0]
    for k in range(1, col_size):
        message = messages[k - 1]
        message[part : part + angles, :] = surf_rhs[...]
        for sub in range(subs):
            at = part + angles + sub * bs
            message[at : at + bs, sub * bs : (sub + 1) * bs] = surf_inverse[sub]


def to_scalars(tables, held, sems):
    copies = [
        pltpu.make_async_copy(table, to, sems.at[i])
        for i, (table, to) in enumerate(zip(tables, held, strict=True))
    ]
    for c in copies:
        c.start()
    return copies


def add_received(total, received):
    for r in received:
        total = total + r[-total.shape[0] :, :].astype(F32)
    return total


def integral_kernel(row_size, vol_size, col_size, refs):
    pair = pair_size(row_size)
    groups = refs[row_size - pair : row_size][::-1] + refs[: row_size - pair]
    refs = refs[row_size:]
    dense, own_trace, *received, _, parts, message = refs
    angles, width = own_trace.shape
    field = jnp.concatenate(
        [g[k * angles : (k + 1) * angles, :] for g in groups for k in range(vol_size)], axis=1
    )
    part = by_cols(field, dense[...])
    for k in range(col_size):
        rows = slice(k * angles, (k + 1) * angles)
        term = part[:, k * width : (k + 1) * width]
        if k == 0:
            term = term + add_received(own_trace[...], received)
        parts[rows, :] = term
        message[rows, :] = term.astype(HALF)


def step_kernel(col_size, refs):
    parts, surf_rhs, surf_inverse, total, *refs = refs
    neighbours, refs = refs[: col_size - 1], refs[col_size - 1 :]
    messages, refs = refs[: col_size - 1], refs[col_size - 1 :]
    surface, half, next_trace, *payloads = refs
    angles = surf_rhs.shape[0]
    bs = surf_inverse.shape[-1]
    subs = surf_inverse.shape[0]
    for j in range(col_size):
        taken = parts[j * angles : (j + 1) * angles, :]
        for shift, message in enumerate(messages, 1):
            k = (j + shift) % col_size
            taken = taken + message[k * angles : (k + 1) * angles, :].astype(F32)
        source = None if j == 0 else neighbours[col_size - j - 1]
        first = 0 if j == 0 else source.shape[0] - angles - subs * bs
        for sub in range(subs):
            cols = slice(sub * bs, (sub + 1) * bs)
            if j == 0:
                rhs, inverse = surf_rhs[:, cols], surf_inverse[sub]
            else:
                at = first + angles + sub * bs
                rhs, inverse = source[first : first + angles, cols], source[at : at + bs, cols]
            resid = (rhs.astype(F32) - taken[:, cols]).astype(HALF)
            value = by_rows(rhs, inverse) + by_rows(resid, inverse)
            if j == 0:
                surface[:, cols] = value
            half[j * angles : (j + 1) * angles, cols] = value.astype(HALF)
    next_trace[...] = total[0]
    send_out(payloads, half[...], total)


def last_integral_kernel(pair, vol_size, col_size, chips, refs):
    groups, refs = refs[:pair], refs[pair:]
    dense, refs = refs[0], refs[1:]
    blocks, outs = refs[: chips * col_size - 1], refs[chips * col_size - 1 :][-chips:]
    angles, width = outs[0].shape
    part = dense.shape[0] // chips
    total = jnp.zeros((angles, chips * width), F32)
    for b in range(col_size):
        place = (col_size - b) % col_size
        field = []
        for g in groups:
            for k in range(vol_size):
                at = (k * col_size + place) * angles
                field.append(g[at : at + angles, :])
        matrix = []
        for a in range(chips):
            own = a == 0 and b == 0
            source = dense if own else blocks[a * col_size + b - 1]
            matrix.append(source[0:part, 0:width])
        total = total + by_cols(
            jnp.concatenate(field, axis=1), jnp.concatenate(matrix, axis=1)
        )
    for a, out in enumerate(outs):
        out[...] = total[:, a * width : (a + 1) * width].astype(out.dtype)


def last_kernel(sums, refs):
    surface, surf_rhs, surf_inverse, integral, own_trace, *refs = refs
    sums, received, out = refs[:sums], refs[sums:-1], refs[-1]
    bs = surf_inverse.shape[-1]
    taken = add_received(integral[...] + own_trace[...], received)
    for s in sums:
        taken = taken + s[...].astype(F32)
    resid = (surf_rhs[...].astype(F32) - taken).astype(HALF)
    for b in range(surf_inverse.shape[0]):
        cols = slice(b * bs, (b + 1) * bs)
        out[:, cols] = surface[:, cols] + by_rows(resid[:, cols], surf_inverse[b])


VMEM = pl.BlockSpec(memory_space=pltpu.VMEM)
SMEM = pl.BlockSpec(memory_space=pltpu.SMEM)


ANY = pl.BlockSpec(memory_space=pl.ANY)
HBM = pl.BlockSpec(memory_space=pltpu.HBM)


def call(body, name, in_specs, outs, flops, moved, scratch=()):
    def kernel(*refs):
        body(refs)

    return pl.pallas_call(
        kernel,
        name=name,
        out_shape=outs,
        in_specs=in_specs,
        out_specs=[VMEM] * len(outs),
        scratch_shapes=list(scratch),
        cost_estimate=pl.CostEstimate(flops=flops, bytes_accessed=moved, transcendentals=0),
        compiler_params=pltpu.CompilerParams(vmem_limit_bytes=48 << 20),
    )


def in_hbm(operand):
    return pltpu.with_memory_space_constraint(operand, pltpu.HBM)


def shifted(value, axis, shift):
    size = lax.axis_size(axis)
    return lax.ppermute(value, axis, [(i, (i + shift) % size) for i in range(size)])


def shifted_in_plane(value, chip, core=0, col=0):
    rows, cols = lax.axis_size("row"), lax.axis_size("col")
    pair = pair_size(rows)
    chips = rows // pair
    pairs = []
    for r in range(rows):
        to = (r // pair + chip) % chips * pair + (r % pair + core) % pair
        pairs += [(r * cols + c, to * cols + (c + col) % cols) for c in range(cols)]
    return lax.ppermute(value, ("row", "col"), pairs)


def local(
    vol_rhs,
    surf_rhs,
    vol_blocks,
    vol_cols,
    coupling,
    trace_map,
    bnd_count,
    surf_inverse,
    near_blocks,
    near_cols,
    far_u,
    far_v,
):
    angles, width = surf_rhs.shape
    vol_count, terms, bs, _ = vol_blocks.shape
    slots = coupling.shape[0]
    nv, nr, nc = (lax.axis_size(a) for a in ("vol", "row", "col"))
    piece = (angles, width)
    product = 2 * angles * bs * bs

    def shape(dims, dtype):
        return jax.ShapeDtypeStruct(dims, dtype)

    tables = (vol_cols.T, trace_map)
    payload_shapes = [shape((2 * angles, width), HALF)] * (nv - 1)
    start_shapes = [shape(piece, HALF), shape(piece, F32)] + payload_shapes
    totals = pltpu.VMEM((nv,) + piece, F32)
    field = pltpu.VMEM((vol_count, angles, bs), HALF)
    scalars = [pltpu.SMEM(t.shape, jnp.int32) for t in tables] + [pltpu.SemaphoreType.DMA((2,))]

    kept = (near_blocks, near_cols, far_u, far_v)
    loaded = (surf_rhs, surf_inverse, vol_rhs, jax.ShapeDtypeStruct((slots, terms, bs, bs), HALF), coupling)
    started = call(
        functools.partial(start_kernel, "vol", len(start_shapes), len(kept)),
        "start",
        [SMEM] + [HBM] * (7 + len(kept)),
        start_shapes + [pltpu.VMEM(a.shape, a.dtype) for a in loaded + tables + kept],
        product * slots * (terms + 1),
        2 * bs * bs * slots * (terms + 1),
        [
            *(pltpu.SMEM(t.shape, jnp.int32) for t in tables),
            totals,
            pltpu.SemaphoreType.DMA((8 + slots + len(kept),)),
        ],
    )(bnd_count, *map(in_hbm, (surf_rhs, surf_inverse, vol_rhs, vol_blocks, coupling) + tables + kept))
    half, own_trace, *payloads = started[: len(start_shapes)]
    surf_rhs, surf_inverse, vol_rhs, boundary_blocks, coupling, *kept = started[len(start_shapes) :]
    tables, kept = (*kept[:2], bnd_count), (*kept[2:], surf_rhs, surf_inverse)

    pair = pair_size(nr)
    chips = nr // pair
    part = nv * pair * width
    sizes = [
        part + (angles + surf_inverse.shape[0] * bs if a == 0 else 0)
        for a in range(chips)
        for b in range(nc)
    ]
    dense, *messages = call(
        functools.partial(dense_kernel, nv, nr, nc),
        "dense",
        [VMEM] * 6,
        [shape((nv * nr * width, nc * width), HALF)]
        + [shape((size, width), HALF) for size in sizes[1:nc]],
        product * nv * nr * nc,
        4 * nv * nr * nc * bs * bs,
        [
            pltpu.SMEM(near_cols.shape, jnp.int32),
            pltpu.SemaphoreType.DMA((1,)),
        ],
    )(*kept)

    messages += [
        dense[i // nc * part : (i // nc + 1) * part, i % nc * width : (i % nc + 1) * width]
        for i in range(nc, nc * chips)
    ]

    received = [shifted(payloads[k - 1], "vol", k) for k in range(1, nv)]
    blocks = [
        shifted_in_plane(messages[i - 1], chip=-(i // nc), col=i % nc) for i in range(1, nc)
    ]
    group = jnp.concatenate([half] + [r[:angles] for r in received], axis=0)
    group, dense = lax.optimization_barrier((group, dense))
    groups = [group] + [
        shifted_in_plane(group, chip=i // pair, core=i % pair) for i in range(1, nr)
    ]
    (total,) = call(
        functools.partial(boundary_kernel, "vol"),
        "boundary",
        [VMEM] * 6 + [SMEM],
        [shape((nv,) + piece, F32)],
        product * slots * (terms + 2),
        2 * bs * bs * slots * (terms + 1),
        [field] + scalars,
    )(group, vol_rhs, boundary_blocks, coupling, *tables)
    ahead = [
        shifted_in_plane(messages[i - 1], chip=-(i // nc), col=0) for i in range(nc, nc * chips, nc)
    ]
    parts, message = call(
        functools.partial(integral_kernel, nr, nv, nc),
        "integral",
        [VMEM] * (nr + nv + 1) + [ANY],
        [shape((nc * angles, width), F32), shape((nc * angles, width), HALF)],
        INTEGRAL_COST,
        2 * nv * nr * nc * width * width,
    )(*groups[pair:], *groups[:pair][::-1], dense, own_trace, *received, total)
    sums = [shifted(message, "col", k) for k in range(1, nc)]
    parts, vol_blocks, *later = lax.optimization_barrier(
        (parts, vol_blocks, *(messages[i - 1] for i in range(nc, nc * chips) if i % nc))
    )
    later = iter(later)
    after = {
        i: shifted_in_plane(next(later), chip=-(i // nc), col=i % nc)
        for i in range(nc, nc * chips)
        if i % nc
    }
    surface, half, own_trace, *payloads = call(
        functools.partial(step_kernel, nc),
        "step",
        [VMEM] * (4 + 2 * (nc - 1)),
        [shape(piece, F32), shape((nc * angles, width), HALF), shape(piece, F32)]
        + [shape(((nc + 1) * angles, width), HALF)] * (nv - 1),
        STEP_COST,
        nc << 17,
    )(parts, surf_rhs, surf_inverse, total, *blocks, *sums)

    received = [shifted(payloads[k - 1], "vol", k) for k in range(1, nv)]
    received, ahead = lax.optimization_barrier((received[:1] + received[:0:-1], ahead))
    received = received[:1] + received[:0:-1]
    half, vol_blocks = lax.optimization_barrier((half, vol_blocks))
    base, matrix = call(
        base_kernel,
        "base_volume",
        [VMEM] * 3,
        [
            shape((angles, vol_count * bs), F32),
            shape((vol_count * bs, (slots + 1) * bs), HALF),
        ],
        product * vol_count * terms,
        2 * bs * bs * vol_count * terms,
        [scalars[0], pltpu.SemaphoreType.DMA((1,))],
    )(vol_rhs, vol_blocks, tables[0])
    group = jnp.concatenate([half] + [r[: nc * angles] for r in received], axis=0)
    group, after = lax.optimization_barrier((group, after))
    blocks += [
        after[i] if i % nc else ahead[i // nc - 1] for i in range(nc, nc * chips)
    ]
    group, base = lax.optimization_barrier((group, base))
    groups = [group] + [shifted_in_plane(group, chip=0, core=k) for k in range(1, pair)]
    integral, *parts = call(
        functools.partial(last_integral_kernel, pair, nv, nc, chips),
        "last_integral",
        [VMEM] * (pair + chips * nc),
        [shape(piece, F32)] + [shape(piece, HALF)] * (chips - 1),
        product * nv * nr * nc,
        2 * nv * nr * nc * width * width,
    )(*groups, dense, *blocks)
    sums = [shifted_in_plane(parts[a - 1], chip=a) for a in range(1, chips)]
    (volume,) = call(
        functools.partial(volume_kernel, "vol", nv, nc),
        "volume",
        [VMEM] * 3 + [SMEM] + [VMEM] * 2,
        [shape((angles, vol_count * bs), F32)],
        product * slots * (vol_count + 1),
        2 * bs * bs * slots * (vol_count + 1),
        [scalars[1], pltpu.SemaphoreType.DMA((1,))],
    )(group, coupling, tables[1], tables[2], base, matrix)
    (surface,) = call(
        functools.partial(last_kernel, chips - 1),
        "last",
        [VMEM] * (5 + chips - 1 + nv - 1),
        [shape(piece, F32)],
        product,
        1 << 17,
    )(surface, surf_rhs, surf_inverse, integral, own_trace, *sums, *received)
    return volume, surface


def solution(mesh):
    everywhere = ("vol", "row", "col")
    in_specs = (
        P(None, everywhere),
        P(None, everywhere),
        P(everywhere, None, None, None),
        P(everywhere, None),
        P(everywhere, None, None),
        P(everywhere),
        P(everywhere),
        P(everywhere, None, None),
        P(("vol", "row"), "col", None, None, None),
        P(("vol", "row"), "col", None),
        P("col", None, ("vol", "row")),
        P(("vol", "row"), "col", None, None),
    )
    out_specs = (P(None, everywhere), P(None, everywhere))
    return jax.shard_map(local, mesh=mesh, in_specs=in_specs, out_specs=out_specs, check_vma=False)
```

```python
import functools

import jax
import jax.numpy as jnp
from jax import lax
from jax.experimental import pallas as pl
from jax.experimental.pallas import tpu as pltpu
from jax.sharding import PartitionSpec as P

UNROLL = 16
INTEGRAL_COST = 10**9
STEP_COST = 10**9
F32 = jnp.float32
HALF = jnp.bfloat16


def by_rows(a, b):
    return lax.dot_general(a, b, (((1,), (1,)), ((), ())), preferred_element_type=F32)


def by_cols(a, b):
    return lax.dot_general(a, b, (((1,), (0,)), ((), ())), preferred_element_type=F32)


def block(start, size):
    return pl.ds(pl.multiple_of(start * size, size), size)


def slot_of(index, here, count):
    return lax.rem(index - here + count, count)


def pair_size(rows):
    return 2 if rows % 2 == 0 else 1


def block_row(read, blocks, columns, row):
    terms = blocks.shape[1]
    field = jnp.concatenate([read(columns[n, row]) for n in range(terms)], axis=1)
    inverse = jnp.concatenate([blocks[row, n] for n in range(terms)], axis=1)
    return by_rows(field, inverse)


def add_traces(total, boundary, coupling, trace_map, bnd_count, axis):
    count = total.shape[0]
    bs = coupling.shape[-1]
    subs = total.shape[2] // bs
    here = lax.axis_index(axis)
    for j in range(coupling.shape[0]):
        alive = (j < bnd_count[0]).astype(F32)
        contrib = by_cols(boundary(j), coupling[j]) * alive
        target = trace_map[j]
        slot = slot_of(target // subs, here, count)
        where = (slot, slice(None), block(lax.rem(target, subs), bs))
        total[where] = total[where] + contrib


def residual_blocks(resid, vol_rhs, group, coupling, trace_map, bnd_count, axis, count, stride):
    bs = coupling.shape[-1]
    angles = vol_rhs.shape[0]
    subs = group.shape[1] // bs
    here = lax.axis_index(axis)
    for j in range(coupling.shape[0]):
        alive = (j < bnd_count[0]).astype(F32)
        target = trace_map[j]
        slot = slot_of(here, target // subs, count)
        picked = group[block(slot * stride, angles), block(lax.rem(target, subs), bs)]
        current = by_rows(picked, coupling[j]) * alive
        rhs = vol_rhs[:, j * bs : (j + 1) * bs].astype(F32)
        resid[j] = (rhs - current).astype(HALF)


def send_out(payloads, half, total):
    rows = half.shape[0]
    for k, payload in enumerate(payloads):
        payload[0:rows, :] = half
        payload[rows:, :] = total[k + 1].astype(HALF)


def start_kernel(axis, outs, kept, refs):
    bnd_count, operands, refs = refs[0], refs[1 : 8 + kept], refs[8 + kept :]
    half_out, own_trace, *payloads = refs[:outs]
    loaded, copied, refs = refs[outs : outs + 5], refs[outs + 5 : outs + 7 + kept], refs[outs + 7 + kept :]
    surf_rhs, surf_inverse, vol_rhs, blocks, coupling = loaded
    columns, trace_map, total, sems = refs
    slots = coupling.shape[0]
    bs = coupling.shape[-1]
    count = iter(range(sems.shape[0]))

    def copy(source, to):
        started = pltpu.make_async_copy(source, to, sems.at[next(count)])
        started.start()
        return started

    tables = [copy(operands[5 + i], t) for i, t in enumerate((columns, trace_map))]
    first = [copy(operands[0], surf_rhs), copy(operands[1], surf_inverse)]
    tables.append(copy(operands[2], vol_rhs))
    rows = [copy(operands[3].at[j], blocks.at[j]) for j in range(slots)]
    last = copy(operands[4], coupling)
    later = [copy(operands[5 + i], t) for i, t in enumerate(copied)]
    total[...] = jnp.zeros_like(total)
    for c in first:
        c.wait()
    for b in range(surf_inverse.shape[0]):
        cols = slice(b * bs, (b + 1) * bs)
        half_out[:, cols] = by_rows(surf_rhs[:, cols], surf_inverse[b]).astype(HALF)
    for c in tables:
        c.wait()
    solved = []
    for j in range(slots):
        rows[j].wait()
        read = lambda col: vol_rhs[:, block(col, bs)]
        solved.append(block_row(read, blocks, columns, j).astype(HALF))
    last.wait()
    add_traces(total, lambda j: solved[j], coupling, trace_map, bnd_count, axis)
    own_trace[...] = total[0]
    send_out(payloads, half_out[...], total)
    for c in later:
        c.wait()


def boundary_kernel(axis, refs):
    group, vol_rhs, blocks, coupling, *tables, bnd_count, total, field, columns, trace_map, sems = refs
    copies = to_scalars(tables, (columns, trace_map), sems)
    bs = coupling.shape[-1]
    slots = coupling.shape[0]
    count = total.shape[0]
    for b in range(slots, vol_rhs.shape[1] // bs):
        field[b] = vol_rhs[:, b * bs : (b + 1) * bs]
    total[...] = jnp.zeros_like(total)
    for c in copies:
        c.wait()
    residual_blocks(field, vol_rhs, group, coupling, trace_map, bnd_count, axis, count, 1)

    def boundary(j):
        return block_row(lambda col: field[col], blocks, columns, j).astype(HALF)

    add_traces(total, boundary, coupling, trace_map, bnd_count, axis)


def early_kernel(axis, count, stride, refs):
    group, vol_rhs, blocks, coupling, *tables, bnd_count, early, field, columns, trace_map, sems = refs
    copies = to_scalars(tables, (columns, trace_map), sems)
    bs = coupling.shape[-1]
    for b in range(coupling.shape[0], vol_rhs.shape[1] // bs):
        field[b] = vol_rhs[:, b * bs : (b + 1) * bs]
    for c in copies:
        c.wait()
    residual_blocks(field, vol_rhs, group, coupling, trace_map, bnd_count, axis, count, stride)
    for b in range(early.shape[1] // bs):
        early[:, b * bs : (b + 1) * bs] = block_row(lambda col: field[col], blocks, columns, b)


def late_kernel(refs):
    early, field, blocks, table, volume, columns, sems = refs
    (copy,) = to_scalars([table], [columns], sems)
    bs = field.shape[-1]
    first = early.shape[1] // bs
    volume[:, : first * bs] = early[...]
    copy.wait()
    for b in range(first, blocks.shape[0]):
        volume[:, b * bs : (b + 1) * bs] = block_row(lambda col: field[col], blocks, columns, b)


def dense_kernel(vol_size, row_size, col_size, refs):
    near_blocks, table, far_u, far_v, surf_rhs, surf_inverse, dense, *messages, near_cols, sems = refs
    (copy,) = to_scalars([table], [near_cols], sems)
    bs = near_blocks.shape[-1]
    rows = near_blocks.shape[0]
    subs = rows // col_size
    pair = pair_size(row_size)
    chips = row_size // pair
    vol, row, col = (lax.axis_index(name) for name in ("vol", "row", "col"))

    def place(number):
        piece = number // subs
        from_row = lax.rem(piece, row_size)
        chip_slot = slot_of(row // pair, from_row // pair, chips)
        pair_slot = slot_of(lax.rem(row, pair), lax.rem(from_row, pair), pair)
        vol_slot = slot_of(vol, piece // row_size, vol_size)
        slot = (chip_slot * pair + pair_slot) * vol_size + vol_slot
        return slot * subs + lax.rem(number, subs)

    total = vol_size * row_size * subs
    part = total * bs // chips
    together = 2 - rows % 2
    for first in range(0, rows, together):
        numbers = [
            lax.rem(col + at // subs, col_size) * subs + at % subs
            for at in range(first, first + together)
        ]
        u = jnp.concatenate([far_u[0, :, block(b, bs)] for b in numbers], axis=1)
        cols = slice(first * bs, (first + together) * bs)

        def far(number, _):
            v = far_v[0, 0, :, block(number, bs)]
            dense[block(place(number), bs), cols] = lax.dot_general(
                v, u, (((0,), (0,)), ((), ())), preferred_element_type=F32
            ).astype(HALF)
            return _

        lax.fori_loop(0, total, far, 0, unroll=min(total, UNROLL))
        if first == 0:
            copy.wait()
        for i, b in enumerate(numbers):
            cols = slice((first + i) * bs, (first + i + 1) * bs)
            for n in range(near_blocks.shape[2]):
                where = (block(place(near_cols[b, 0, n]), bs), cols)
                near = near_blocks[b, 0, n].astype(F32).T
                dense[where] = (dense[where].astype(F32) + near).astype(HALF)
    width = subs * bs
    for k in range(1, col_size):
        messages[k - 1][0:part, :] = dense[0:part, k * width : (k + 1) * width]
    angles = surf_rhs.shape[0]
    for k in range(1, col_size):
        message = messages[k - 1]
        message[part : part + angles, :] = surf_rhs[...]
        for sub in range(subs):
            at = part + angles + sub * bs
            message[at : at + bs, sub * bs : (sub + 1) * bs] = surf_inverse[sub]


def to_scalars(tables, held, sems):
    copies = [
        pltpu.make_async_copy(table, to, sems.at[i])
        for i, (table, to) in enumerate(zip(tables, held, strict=True))
    ]
    for c in copies:
        c.start()
    return copies


def add_received(total, received):
    for r in received:
        total = total + r[-total.shape[0] :, :].astype(F32)
    return total


def integral_kernel(row_size, vol_size, col_size, refs):
    pair = pair_size(row_size)
    groups = refs[row_size - pair : row_size][::-1] + refs[: row_size - pair]
    refs = refs[row_size:]
    dense, own_trace, *received, _, parts, message = refs
    angles, width = own_trace.shape
    field = jnp.concatenate(
        [g[k * angles : (k + 1) * angles, :] for g in groups for k in range(vol_size)], axis=1
    )
    part = by_cols(field, dense[...])
    for k in range(col_size):
        rows = slice(k * angles, (k + 1) * angles)
        term = part[:, k * width : (k + 1) * width]
        if k == 0:
            term = term + add_received(own_trace[...], received)
        parts[rows, :] = term
        message[rows, :] = term.astype(HALF)


def step_kernel(col_size, refs):
    parts, surf_rhs, surf_inverse, total, *refs = refs
    neighbours, refs = refs[: col_size - 1], refs[col_size - 1 :]
    messages, refs = refs[: col_size - 1], refs[col_size - 1 :]
    surface, half, next_trace, *payloads = refs
    angles = surf_rhs.shape[0]
    bs = surf_inverse.shape[-1]
    subs = surf_inverse.shape[0]
    for j in range(col_size):
        taken = parts[j * angles : (j + 1) * angles, :]
        for shift, message in enumerate(messages, 1):
            k = (j + shift) % col_size
            taken = taken + message[k * angles : (k + 1) * angles, :].astype(F32)
        source = None if j == 0 else neighbours[col_size - j - 1]
        first = 0 if j == 0 else source.shape[0] - angles - subs * bs
        for sub in range(subs):
            cols = slice(sub * bs, (sub + 1) * bs)
            if j == 0:
                rhs, inverse = surf_rhs[:, cols], surf_inverse[sub]
            else:
                at = first + angles + sub * bs
                rhs, inverse = source[first : first + angles, cols], source[at : at + bs, cols]
            resid = (rhs.astype(F32) - taken[:, cols]).astype(HALF)
            value = by_rows(rhs, inverse) + by_rows(resid, inverse)
            if j == 0:
                surface[:, cols] = value
            half[j * angles : (j + 1) * angles, cols] = value.astype(HALF)
    next_trace[...] = total[0]
    send_out(payloads, half[...], total)


def last_integral_kernel(pair, vol_size, col_size, chips, refs):
    groups, refs = refs[:pair], refs[pair:]
    dense, refs = refs[0], refs[1:]
    blocks, outs = refs[: chips * col_size - 1], refs[chips * col_size - 1 :][-chips:]
    angles, width = outs[0].shape
    part = dense.shape[0] // chips
    total = jnp.zeros((angles, chips * width), F32)
    for b in range(col_size):
        place = (col_size - b) % col_size
        field = []
        for g in groups:
            for k in range(vol_size):
                at = (k * col_size + place) * angles
                field.append(g[at : at + angles, :])
        matrix = []
        for a in range(chips):
            own = a == 0 and b == 0
            source = dense if own else blocks[a * col_size + b - 1]
            matrix.append(source[0:part, 0:width])
        total = total + by_cols(
            jnp.concatenate(field, axis=1), jnp.concatenate(matrix, axis=1)
        )
    for a, out in enumerate(outs):
        out[...] = total[:, a * width : (a + 1) * width].astype(out.dtype)


def last_kernel(sums, refs):
    surface, surf_rhs, surf_inverse, integral, own_trace, *refs = refs
    sums, received, out = refs[:sums], refs[sums:-1], refs[-1]
    bs = surf_inverse.shape[-1]
    taken = add_received(integral[...] + own_trace[...], received)
    for s in sums:
        taken = taken + s[...].astype(F32)
    resid = (surf_rhs[...].astype(F32) - taken).astype(HALF)
    for b in range(surf_inverse.shape[0]):
        cols = slice(b * bs, (b + 1) * bs)
        out[:, cols] = surface[:, cols] + by_rows(resid[:, cols], surf_inverse[b])


VMEM = pl.BlockSpec(memory_space=pltpu.VMEM)
SMEM = pl.BlockSpec(memory_space=pltpu.SMEM)


ANY = pl.BlockSpec(memory_space=pl.ANY)
HBM = pl.BlockSpec(memory_space=pltpu.HBM)


def call(body, name, in_specs, outs, flops, moved, scratch=()):
    def kernel(*refs):
        body(refs)

    return pl.pallas_call(
        kernel,
        name=name,
        out_shape=outs,
        in_specs=in_specs,
        out_specs=[VMEM] * len(outs),
        scratch_shapes=list(scratch),
        cost_estimate=pl.CostEstimate(flops=flops, bytes_accessed=moved, transcendentals=0),
        compiler_params=pltpu.CompilerParams(vmem_limit_bytes=48 << 20),
    )


def in_hbm(operand):
    return pltpu.with_memory_space_constraint(operand, pltpu.HBM)


def shifted(value, axis, shift):
    size = lax.axis_size(axis)
    return lax.ppermute(value, axis, [(i, (i + shift) % size) for i in range(size)])


def shifted_in_plane(value, chip, core=0, col=0):
    rows, cols = lax.axis_size("row"), lax.axis_size("col")
    pair = pair_size(rows)
    chips = rows // pair
    pairs = []
    for r in range(rows):
        to = (r // pair + chip) % chips * pair + (r % pair + core) % pair
        pairs += [(r * cols + c, to * cols + (c + col) % cols) for c in range(cols)]
    return lax.ppermute(value, ("row", "col"), pairs)


def local(
    vol_rhs,
    surf_rhs,
    vol_blocks,
    vol_cols,
    coupling,
    trace_map,
    bnd_count,
    surf_inverse,
    near_blocks,
    near_cols,
    far_u,
    far_v,
):
    angles, width = surf_rhs.shape
    vol_count, terms, bs, _ = vol_blocks.shape
    slots = coupling.shape[0]
    nv, nr, nc = (lax.axis_size(a) for a in ("vol", "row", "col"))
    piece = (angles, width)
    product = 2 * angles * bs * bs

    def shape(dims, dtype):
        return jax.ShapeDtypeStruct(dims, dtype)

    tables = (vol_cols.T, trace_map)
    payload_shapes = [shape((2 * angles, width), HALF)] * (nv - 1)
    start_shapes = [shape(piece, HALF), shape(piece, F32)] + payload_shapes
    totals = pltpu.VMEM((nv,) + piece, F32)
    field = pltpu.VMEM((vol_count, angles, bs), HALF)
    scalars = [pltpu.SMEM(t.shape, jnp.int32) for t in tables] + [pltpu.SemaphoreType.DMA((2,))]

    kept = (near_blocks, near_cols, far_u, far_v)
    loaded = (surf_rhs, surf_inverse, vol_rhs, jax.ShapeDtypeStruct((slots, terms, bs, bs), HALF), coupling)
    started = call(
        functools.partial(start_kernel, "vol", len(start_shapes), len(kept)),
        "start",
        [SMEM] + [HBM] * (7 + len(kept)),
        start_shapes + [pltpu.VMEM(a.shape, a.dtype) for a in loaded + tables + kept],
        product * slots * (terms + 1),
        2 * bs * bs * slots * (terms + 1),
        [
            *(pltpu.SMEM(t.shape, jnp.int32) for t in tables),
            totals,
            pltpu.SemaphoreType.DMA((8 + slots + len(kept),)),
        ],
    )(bnd_count, *map(in_hbm, (surf_rhs, surf_inverse, vol_rhs, vol_blocks, coupling) + tables + kept))
    half, own_trace, *payloads = started[: len(start_shapes)]
    surf_rhs, surf_inverse, vol_rhs, boundary_blocks, coupling, *kept = started[len(start_shapes) :]
    tables, kept = (*kept[:2], bnd_count), (*kept[2:], surf_rhs, surf_inverse)

    pair = pair_size(nr)
    chips = nr // pair
    part = nv * pair * width
    sizes = [
        part + (angles + surf_inverse.shape[0] * bs if a == 0 else 0)
        for a in range(chips)
        for b in range(nc)
    ]
    dense, *messages = call(
        functools.partial(dense_kernel, nv, nr, nc),
        "dense",
        [VMEM] * 6,
        [shape((nv * nr * width, nc * width), HALF)]
        + [shape((size, width), HALF) for size in sizes[1:nc]],
        product * nv * nr * nc,
        4 * nv * nr * nc * bs * bs,
        [
            pltpu.SMEM(near_cols.shape, jnp.int32),
            pltpu.SemaphoreType.DMA((1,)),
        ],
    )(*kept)

    messages += [
        dense[i // nc * part : (i // nc + 1) * part, i % nc * width : (i % nc + 1) * width]
        for i in range(nc, nc * chips)
    ]

    received = [shifted(payloads[k - 1], "vol", k) for k in range(1, nv)]
    blocks = [
        shifted_in_plane(messages[i - 1], chip=-(i // nc), col=i % nc) for i in range(1, nc)
    ]
    group = jnp.concatenate([half] + [r[:angles] for r in received], axis=0)
    group, dense = lax.optimization_barrier((group, dense))
    groups = [group] + [
        shifted_in_plane(group, chip=i // pair, core=i % pair) for i in range(1, nr)
    ]
    (total,) = call(
        functools.partial(boundary_kernel, "vol"),
        "boundary",
        [VMEM] * 6 + [SMEM],
        [shape((nv,) + piece, F32)],
        product * slots * (terms + 2),
        2 * bs * bs * slots * (terms + 1),
        [field] + scalars,
    )(group, vol_rhs, boundary_blocks, coupling, *tables)
    ahead = [
        shifted_in_plane(messages[i - 1], chip=-(i // nc), col=0) for i in range(nc, nc * chips, nc)
    ]
    parts, message = call(
        functools.partial(integral_kernel, nr, nv, nc),
        "integral",
        [VMEM] * (nr + nv + 1) + [ANY],
        [shape((nc * angles, width), F32), shape((nc * angles, width), HALF)],
        INTEGRAL_COST,
        2 * nv * nr * nc * width * width,
    )(*groups[pair:], *groups[:pair][::-1], dense, own_trace, *received, total)
    sums = [shifted(message, "col", k) for k in range(1, nc)]
    parts, vol_blocks, *later = lax.optimization_barrier(
        (parts, vol_blocks, *(messages[i - 1] for i in range(nc, nc * chips) if i % nc))
    )
    later = iter(later)
    after = {
        i: shifted_in_plane(next(later), chip=-(i // nc), col=i % nc)
        for i in range(nc, nc * chips)
        if i % nc
    }
    surface, half, own_trace, *payloads = call(
        functools.partial(step_kernel, nc),
        "step",
        [VMEM] * (4 + 2 * (nc - 1)),
        [shape(piece, F32), shape((nc * angles, width), HALF), shape(piece, F32)]
        + [shape(((nc + 1) * angles, width), HALF)] * (nv - 1),
        STEP_COST,
        nc << 17,
    )(parts, surf_rhs, surf_inverse, total, *blocks, *sums)

    received = [shifted(payloads[k - 1], "vol", k) for k in range(1, nv)]
    received, ahead = lax.optimization_barrier((received[1:] + received[:1], ahead))
    received = received[-1:] + received[:-1]
    group = jnp.concatenate([half] + [r[: nc * angles] for r in received], axis=0)
    group, after = lax.optimization_barrier((group, after))
    blocks += [
        after[i] if i % nc else ahead[i // nc - 1] for i in range(nc, nc * chips)
    ]
    groups = [group] + [shifted_in_plane(group, chip=0, core=k) for k in range(1, pair)]
    split = vol_count // 3
    early, residual = call(
        functools.partial(early_kernel, "vol", nv, nc),
        "early_volume",
        [VMEM] * 6 + [SMEM],
        [shape((angles, split * bs), F32), shape((vol_count, angles, bs), HALF)],
        product * split * terms,
        2 * bs * bs * split * terms,
        scalars,
    )(group, vol_rhs, vol_blocks, coupling, *tables)
    integral, *parts = call(
        functools.partial(last_integral_kernel, pair, nv, nc, chips),
        "last_integral",
        [VMEM] * (pair + chips * nc) + [ANY],
        [shape(piece, F32)] + [shape(piece, HALF)] * (chips - 1),
        product * nv * nr * nc,
        2 * nv * nr * nc * width * width,
    )(*groups, dense, *blocks, early)
    sums = [shifted_in_plane(parts[a - 1], chip=a) for a in range(1, chips)]
    (volume,) = call(
        late_kernel,
        "late_volume",
        [VMEM] * 4,
        [shape((angles, vol_count * bs), F32)],
        product * (vol_count - split) * terms,
        2 * bs * bs * (vol_count - split) * terms,
        [scalars[0], pltpu.SemaphoreType.DMA((1,))],
    )(early, residual, vol_blocks, tables[0])
    (surface,) = call(
        functools.partial(last_kernel, chips - 1),
        "last",
        [VMEM] * (5 + chips - 1 + nv - 1),
        [shape(piece, F32)],
        product,
        1 << 17,
    )(surface, surf_rhs, surf_inverse, integral, own_trace, *sums, *received)
    return volume, surface


def solution(mesh):
    everywhere = ("vol", "row", "col")
    in_specs = (
        P(None, everywhere),
        P(None, everywhere),
        P(everywhere, None, None, None),
        P(everywhere, None),
        P(everywhere, None, None),
        P(everywhere),
        P(everywhere),
        P(everywhere, None, None),
        P(("vol", "row"), "col", None, None, None),
        P(("vol", "row"), "col", None),
        P("col", None, ("vol", "row")),
        P(("vol", "row"), "col", None, None),
    )
    out_specs = (P(None, everywhere), P(None, everywhere))
    return jax.shard_map(local, mesh=mesh, in_specs=in_specs, out_specs=out_specs, check_vma=False)
```
